32 devices in a mesh: groups: 2 (over x), seq: 16 (over z, y, core).
Axes of the slice: x: 2, y: 2, z: 4, core: 2. Of those that a mesh axis runs over, the one named last changes fastest.
Arguments:
- signal: bfloat16 [16384, 2048], P(('groups', 'seq')), parts along dimension 0, may hold values from -6 to 6
- gate_input: bfloat16 [16384, 2048], P(('groups', 'seq')), parts along dimension 0, may hold values from -6 to 6
- cotangent: bfloat16 [16384, 2048], P(('groups', 'seq')), parts along dimension 0, may hold values from -6 to 6
- block_factor: bfloat16 [512, 512], replicated, may hold values from -0.25 to 0.25
- cross_factor: bfloat16 [512, 16, 16], P('seq'), may hold values from -1.5 to 1.5
- order_table: int32 [512], replicated, may hold values from 0 to 511, each once
Outputs:
- grad_signal: bfloat16 [16384, 2048], P(('groups', 'seq')), parts along dimension 0
- grad_gate: bfloat16 [16384, 2048], P(('groups', 'seq')), parts along dimension 0
- grad_block: float32 [1024, 512], P('groups'), parts along dimension 0
- grad_cross: float32 [512, 32, 16], P('seq', 'groups'), parts along dimension 1
The draws below stay inside these ranges and needn't reach their ends.
There are 2 independent parts, one for each index of `groups`. The reference program is written for one: setup_inputs(seed, part) draws one part's arguments, and reference() takes and returns one part's arrays. A program takes and returns all parts, laid end to end along the dimension named above; an argument that names none is the same for every part. Nothing has to cross between parts.
Inputs may be any that keep to these rules, and one draw needn't show every extreme that they name: order_table holds every number of 0 to 511 exactly once.
All inputs are finite; a program needn't handle non-finite values.
Results may differ from the reference program's by a relative error of at most 0.0057.
Values may be sent and summed in bfloat16 or wider, within the bound.
No kernel may reach another device: no remote copies, remote signals or barrier semaphores. Data moves between devices by JAX's collectives and lax.ppermute only.
A program may use at most 64 MiB of HBM per device.

```python
import math
import jax
import jax.numpy as jnp

BLOCK = 512
WIDTH = 2048
BLOCKS = 16
TOKENS = 8192


def shard_levels(key, extent, split, low, top_value):
    gain, own = 1.0, jax.random.fold_in(key, 6)
    for axis_at, parts in split:
        heights = jnp.exp(jax.random.uniform(jax.random.fold_in(own, axis_at), (parts,), jnp.float32, low / len(split), top_value / len(split)))
        gain = gain * jnp.repeat(heights, extent[axis_at] // parts).reshape([-1 if axis == axis_at else 1 for axis in range(len(extent))])
    return gain


def gaussian(key, shape, deviation, reach, pieces=(), dtype=jnp.bfloat16):
    gain = shard_levels(key, shape, pieces, -0.22, 0.18) if pieces else 1.0
    entries = jax.random.normal(key, shape, jnp.float32) * deviation * gain
    return jnp.minimum(jnp.maximum(entries, -reach), reach).astype(dtype)


def setup_inputs(seed: int = 0, part: int = 0) -> dict:
    key_list = jax.random.split(jax.random.key(seed), 7)
    own_keys = jax.random.split(jax.random.fold_in(key_list[6], part), 7)
    signal = gaussian(own_keys[0], (TOKENS, WIDTH), 1.0, 6.0, ((0, 16),))
    gate_input = gaussian(own_keys[1], (TOKENS, WIDTH), 1.0, 6.0, ((0, 16),))
    cotangent = gaussian(own_keys[2], (TOKENS, WIDTH), 1.0, 6.0, ((0, 16),))
    block_factor = gaussian(key_list[3], (BLOCK, BLOCK), BLOCK ** -0.5, 0.25)
    cross_factor = gaussian(key_list[4], (BLOCK, BLOCKS, BLOCKS), BLOCKS ** -0.5, 1.5, ((0, 16),))
    order_table = jax.random.permutation(key_list[5], BLOCK).astype(jnp.int32)
    return dict(signal=signal, gate_input=gate_input, cotangent=cotangent, block_factor=block_factor, cross_factor=cross_factor, order_table=order_table)


def reference(signal, gate_input, cotangent, block_factor, cross_factor, order_table):
    f32 = jnp.float32
    bf16 = jnp.bfloat16
    source = signal.reshape(BLOCKS, BLOCK, WIDTH)
    permuted = source[:, order_table, :]
    block_w = block_factor.astype(f32)
    cross_w = cross_factor.astype(f32)
    mixed = jnp.einsum('cb,abd->acd', block_w, permuted.astype(f32)).astype(bf16)
    gated = jnp.einsum('cij,jcd->icd', cross_w, mixed.astype(f32)).astype(bf16)
    cot = cotangent.astype(f32)
    gate_grad = (cot * gate_input.astype(f32)).astype(bf16).reshape(BLOCKS, BLOCK, WIDTH)
    grad_gate = (cot * gated.reshape(TOKENS, WIDTH).astype(f32)).astype(bf16)
    grad_cross = jnp.einsum('icd,jcd->cij', gate_grad.astype(f32), mixed.astype(f32)) / math.sqrt(WIDTH)
    back = jnp.einsum('cij,icd->jcd', cross_w, gate_grad.astype(f32)).astype(bf16)
    grad_block = jnp.einsum('acd,abd->cb', back.astype(f32), permuted.astype(f32)) / math.sqrt(BLOCKS * WIDTH)
    spread = jnp.einsum('cb,acd->abd', block_w, back.astype(f32)).astype(bf16)
    grad_signal = jnp.zeros_like(spread).at[:, order_table, :].set(spread).reshape(TOKENS, WIDTH)
    return (grad_signal, grad_gate, grad_block, grad_cross)
```

```python
import math

import jax
import jax.numpy as jnp
from jax import lax
from jax.sharding import PartitionSpec as P


def exchange(rows):
    return lax.all_to_all(rows, "seq", split_axis=0, concat_axis=0, tiled=True)


def per_device(signal, gate_input, cotangent, block_factor, cross_factor, order_table):
    f32 = jnp.float32
    bf16 = jnp.bfloat16
    count = lax.axis_size("seq")
    block, width = signal.shape
    share = block // count
    parted = (count, share, width)
    gate_grad = (cotangent.astype(f32) * gate_input.astype(f32)).astype(bf16)
    spread_grad = exchange(gate_grad.reshape(parted))

    one_hot = (order_table[:, None] == jnp.arange(block, dtype=jnp.int32)[None, :]).astype(bf16)
    factor = jnp.dot(block_factor, one_hot, preferred_element_type=f32).astype(bf16)
    mixed = jnp.dot(factor, signal, preferred_element_type=f32).astype(bf16)

    back = jnp.einsum("cij,icd->jcd", cross_factor, spread_grad, preferred_element_type=f32).astype(
        bf16
    )
    back, mixed = lax.optimization_barrier((back, mixed))
    back_rows = exchange(back).reshape(block, width)
    back_rows, mixed = lax.optimization_barrier((back_rows, mixed))
    spread_mixed = exchange(mixed.reshape(parted))

    partial_block = lax.dot_general(
        back_rows, signal, (((1,), (1,)), ((), ())), preferred_element_type=f32
    )
    partial_block = jnp.dot(
        partial_block.astype(bf16), one_hot.T, preferred_element_type=f32
    )
    grad_block = lax.psum(partial_block, "seq") / math.sqrt(count * width)
    grad_signal = lax.dot_general(
        factor, back_rows, (((0,), (0,)), ((), ())), preferred_element_type=f32
    ).astype(bf16)

    gated = jnp.einsum(
        "cij,jcd->icd", cross_factor, spread_mixed, preferred_element_type=f32
    ).astype(bf16)
    gated_home = exchange(gated).reshape(block, width)
    grad_cross = jnp.einsum(
        "icd,jcd->cij", spread_grad, spread_mixed, preferred_element_type=f32
    ) / math.sqrt(width)
    grad_gate = (cotangent.astype(f32) * gated_home.astype(f32)).astype(bf16)
    return (grad_signal, grad_gate, grad_block, grad_cross)


def solution(mesh):
    in_specs = (
        P(("groups", "seq"), None),
        P(("groups", "seq"), None),
        P(("groups", "seq"), None),
        P(),
        P("seq", None, None),
        P(),
    )
    out_specs = (
        P(("groups", "seq"), None),
        P(("groups", "seq"), None),
        P("groups", None),
        P("seq", "groups", None),
    )
    return jax.shard_map(
        per_device, mesh=mesh, in_specs=in_specs, out_specs=out_specs, check_vma=False
    )
```

```python
import functools
import math

import jax
import jax.numpy as jnp
from jax import lax
from jax.experimental import pallas as pl
from jax.experimental.pallas import tpu as pltpu
from jax.sharding import PartitionSpec as P

F32 = jnp.float32
BF16 = jnp.bfloat16


def order_kernel(scale, position, rows, out):
    for a in range(rows.shape[0]):
        out[a] = rows[position[a]].astype(F32) * scale


def in_order(position, rows, scale):
    return pl.pallas_call(
        functools.partial(order_kernel, scale),
        in_specs=[
            pl.BlockSpec(memory_space=pltpu.SMEM),
            pl.BlockSpec(memory_space=pltpu.VMEM),
        ],
        out_specs=pl.BlockSpec(memory_space=pltpu.VMEM),
        out_shape=jax.ShapeDtypeStruct(rows.shape, F32),
    )(position, rows)


def exchange(rows):
    return lax.all_to_all(rows, "seq", split_axis=0, concat_axis=0, tiled=True)


def near_far():
    count = lax.axis_size("seq")
    inner = min(4, count)
    me = lax.axis_index("seq")

    def across(x, k):
        return lax.ppermute(
            x, "seq", [(s, ((s // inner) ^ k) * inner + s % inner) for s in range(count)]
        )

    def within(x, q):
        return lax.ppermute(
            x, "seq", [(s, s // inner * inner + ((s % inner) ^ q)) for s in range(count)]
        )

    return count // inner, inner, me // inner, me % inner, across, within


def tree_sum(terms):
    terms = [t.astype(F32) for t in terms]
    while len(terms) > 1:
        terms = [a + b for a, b in zip(terms[::2], terms[1::2])]
    return terms[0].astype(BF16)


def reduce_near(terms):
    outer, inner, z, r, across, within = near_far()
    block, n = terms.shape
    terms = terms.reshape(outer, inner, block // (outer * inner), n)
    lane = lambda q: lax.dynamic_index_in_dim(terms, jnp.bitwise_xor(r, q), 1, keepdims=False)
    return tree_sum([lane(0)] + [within(lane(q), q) for q in range(1, inner)])


def reduce_far(half):
    outer, inner, z, r, across, within = near_far()
    plane = lambda k: lax.dynamic_index_in_dim(half, jnp.bitwise_xor(z, k), 0, keepdims=False)
    return tree_sum([plane(0)] + [across(plane(k), k) for k in range(1, outer)])


def gather_far(own):
    outer, inner, z, r, across, within = near_far()
    return [own] + [across(own, k) for k in range(1, outer)]


def gather_near(rows, scale):
    outer, inner, z, r, across, within = near_far()
    got = jnp.stack(rows)
    got = jnp.concatenate([got] + [within(got, q) for q in range(1, inner)])
    every = jnp.arange(outer * inner, dtype=jnp.int32)
    position = jnp.bitwise_xor(r, every % inner) * outer + jnp.bitwise_xor(z, every // inner)
    return in_order(position.astype(jnp.int32), got, scale).reshape(-1, rows[0].shape[-1])


def per_device(signal, gate_input, cotangent, block_factor, cross_factor, order_table):
    count = lax.axis_size("seq")
    block, width = signal.shape
    share = block // count
    parted = (count, share, width)
    gate_grad = cotangent * gate_input
    spread_grad = exchange(gate_grad.reshape(parted))

    one_hot = (order_table[:, None] == jnp.arange(block, dtype=jnp.int32)[None, :]).astype(BF16)
    factor = jnp.dot(block_factor, one_hot, preferred_element_type=F32).astype(BF16)
    every = jnp.arange(block, dtype=jnp.int32)
    blocks = (every[:, None] // share == jnp.arange(count, dtype=jnp.int32)[None, :]).astype(BF16)
    same = every[:, None] % share == every[None, :] % share
    cross = cross_factor.swapaxes(0, 1).reshape(block, count)
    cross = jnp.dot(cross, blocks.T, preferred_element_type=F32)
    cross = jnp.where(same, cross, 0.0).astype(BF16)
    factor, cross, spread_grad = lax.optimization_barrier((factor, cross, spread_grad))

    grad_rows = spread_grad.reshape(block, width)
    back = lax.dot_general(
        cross, grad_rows, (((0,), (0,)), ((), ())), preferred_element_type=F32
    ).astype(BF16)
    factor, back = lax.optimization_barrier((factor, back))
    mixed = jnp.dot(factor, signal, preferred_element_type=F32).astype(BF16)
    back_rows = exchange(back.reshape(parted)).reshape(block, width)
    mixed, back_rows = lax.optimization_barrier((mixed, back_rows))
    spread_mixed = exchange(mixed.reshape(parted))

    partial_block = lax.dot_general(
        back_rows, signal, (((1,), (1,)), ((), ())), preferred_element_type=F32
    ).astype(BF16)
    partial_block = jnp.dot(partial_block, one_hot.T, preferred_element_type=F32).astype(BF16)
    own_block = reduce_far(reduce_near(partial_block))
    spread_mixed, own_block = lax.optimization_barrier((spread_mixed, own_block))
    far_blocks = gather_far(own_block)

    mixed_rows = spread_mixed.reshape(block, width)
    gated = jnp.dot(cross, mixed_rows, preferred_element_type=F32).astype(BF16)
    gated, far_blocks = lax.optimization_barrier((gated, far_blocks))
    gated_home = exchange(gated.reshape(parted)).reshape(block, width)

    grad_block = gather_near(far_blocks, 1.0 / math.sqrt(count * width))
    grad_signal = lax.dot_general(
        factor, back_rows, (((0,), (0,)), ((), ())), preferred_element_type=F32
    ).astype(BF16)
    products = lax.dot_general(
        grad_rows, mixed_rows, (((1,), (1,)), ((), ())), preferred_element_type=F32
    )
    products = jnp.dot(
        jnp.where(same, products, 0.0), blocks.astype(F32), precision=lax.Precision.HIGHEST
    )
    grad_cross = products.reshape(count, share, count).swapaxes(0, 1) / math.sqrt(width)
    gated_home, grad_block, grad_signal, grad_cross = lax.optimization_barrier(
        (gated_home, grad_block, grad_signal, grad_cross)
    )
    grad_gate = cotangent * gated_home
    return (grad_signal, grad_gate, grad_block, grad_cross)


def solution(mesh):
    in_specs = (
        P(("groups", "seq"), None),
        P(("groups", "seq"), None),
        P(("groups", "seq"), None),
        P(),
        P("seq", None, None),
        P(),
    )
    out_specs = (
        P(("groups", "seq"), None),
        P(("groups", "seq"), None),
        P("groups", None),
        P("seq", "groups", None),
    )
    return jax.shard_map(
        per_device, mesh=mesh, in_specs=in_specs, out_specs=out_specs, check_vma=False
    )
```

```python
import functools
import math

import jax
import jax.numpy as jnp
from jax import lax
from jax.experimental import pallas as pl
from jax.experimental.pallas import tpu as pltpu
from jax.sharding import PartitionSpec as P

F32 = jnp.float32
BF16 = jnp.bfloat16
COLUMNS = 512
LIMIT = pltpu.CompilerParams(vmem_limit_bytes=40 * 1024 * 1024)


def split_kernel(share, core, *refs):
    *slabs, keep, send = refs
    mine = core[0] == 0
    at = 0
    for slab in slabs:
        for i in range(0, slab.shape[0], 2 * share):
            low, high = slab[i : i + share], slab[i + share : i + 2 * share]
            keep[at : at + share] = jnp.where(mine, low, high)
            send[at : at + share] = jnp.where(mine, high, low)
            at += share


def join_kernel(share, core, own, other, *slabs):
    mine = core[0] == 0
    at = 0
    for slab in slabs:
        for i in range(0, slab.shape[0], 2 * share):
            a, b = own[at : at + share], other[at : at + share]
            slab[i : i + share] = jnp.where(mine, a, b)
            slab[i + share : i + 2 * share] = jnp.where(mine, b, a)
            at += share


def mix_kernel(matrix, own, other, own_out, other_out):
    rows = jnp.concatenate([own[...], other[...]], axis=0)
    half = own.shape[0]
    own_out[...] = jnp.dot(matrix[:half], rows, preferred_element_type=F32).astype(BF16)
    other_out[...] = jnp.dot(matrix[half:], rows, preferred_element_type=F32).astype(BF16)


def place_kernel(starts, a, *refs):
    *slabs, out = refs
    for i, slab in enumerate(slabs):
        at = pl.ds(pl.multiple_of(starts[i], slab.shape[0]), slab.shape[0])
        out[at] = a[at] * slab[...]


def cut_kernel(matrix, rows, *slabs):
    total = jnp.dot(matrix[...], rows[...], preferred_element_type=F32).astype(BF16)
    at = 0
    for slab in slabs:
        slab[...] = total[at : at + slab.shape[0]]
        at += slab.shape[0]


def whole_kernel(matrix, *refs):
    *slabs, out = refs
    rows = jnp.concatenate([s[...] for s in slabs], axis=0)
    out[...] = jnp.dot(matrix[...], rows, preferred_element_type=F32).astype(BF16)


def partial_kernel(order, right, *refs):
    *slabs, out, total = refs

    @pl.when(pl.program_id(0) == 0)
    def _():
        total[...] = jnp.zeros_like(total)

    left = jnp.concatenate([s[...] for s in slabs], axis=0)
    total[...] += lax.dot_general(
        left, right[...], (((1,), (1,)), ((), ())), preferred_element_type=F32
    )

    @pl.when(pl.program_id(0) == pl.num_programs(0) - 1)
    def _():
        out[...] = jnp.dot(
            order[...], total[...].astype(BF16), preferred_element_type=F32
        ).astype(BF16)


def gradient_kernel(same, spread_out, *refs):
    g, h, m, n, out, total = refs

    @pl.when(pl.program_id(0) == 0)
    def _():
        total[...] = jnp.zeros_like(total)

    left = jnp.concatenate([g[...], h[...]], axis=0)
    right = jnp.concatenate([m[...], n[...]], axis=0)
    total[...] += lax.dot_general(
        left, right, (((1,), (1,)), ((), ())), preferred_element_type=F32
    )

    @pl.when(pl.program_id(0) == pl.num_programs(0) - 1)
    def _():
        out[...] = jnp.dot(
            total[...] * same[...].astype(F32),
            spread_out[...].astype(F32),
            precision=lax.Precision.HIGHEST,
            preferred_element_type=F32,
        )


def order_kernel(scale, position, *refs):
    *parts, out = refs
    at = 0
    for rows in parts:
        for i in range(rows.shape[0]):
            out[position[at]] = rows[i].astype(F32) * scale
            at += 1


def by_columns(kernel, ins, outs, width, scalars=(), whole=(), scratch=(), dtype=BF16):
    columns = min(COLUMNS, width)
    block = lambda rows: pl.BlockSpec((rows, columns), lambda i: (0, i))
    full = lambda shape: pl.BlockSpec(shape, lambda i: (0, 0))
    return pl.pallas_call(
        kernel,
        grid=(width // columns,),
        in_specs=[pl.BlockSpec(memory_space=pltpu.SMEM) for _ in scalars]
        + [full(x.shape) for x in whole]
        + [block(x.shape[0]) for x in ins],
        out_specs=[block(n) if isinstance(n, int) else full(n) for n in outs],
        out_shape=[
            jax.ShapeDtypeStruct((n, width) if isinstance(n, int) else n, dtype) for n in outs
        ],
        scratch_shapes=list(scratch),
        compiler_params=LIMIT,
    )(*scalars, *whole, *ins)


def in_order(position, parts, scale):
    _, share, n = parts[0].shape
    return pl.pallas_call(
        functools.partial(order_kernel, scale),
        in_specs=[pl.BlockSpec(memory_space=pltpu.SMEM)]
        + [pl.BlockSpec(memory_space=pltpu.VMEM) for _ in parts],
        out_specs=pl.BlockSpec(memory_space=pltpu.VMEM),
        out_shape=jax.ShapeDtypeStruct((sum(x.shape[0] for x in parts), share, n), F32),
        compiler_params=LIMIT,
    )(position, *parts)


def tree_sum(terms):
    terms = [t.astype(F32) for t in terms]
    while len(terms) > 1:
        terms = [a + b for a, b in zip(terms[::2], terms[1::2])]
    return terms[0].astype(BF16)


def per_device(signal, gate_input, cotangent, block_factor, cross_factor, order_table):
    count = lax.axis_size("seq")
    block, width = signal.shape
    share = block // count
    chips, slab = count // 2, 2 * share
    far = chips // 2
    me = lax.axis_index("seq")
    h, e = me // 2, me % 2
    core = e.reshape(1).astype(jnp.int32)
    true = order_table[0] >= 0

    def phase(f, *args):
        shapes = jax.eval_shape(f, *args)
        none = lambda *a: jax.tree.map(lambda s: jnp.zeros(s.shape, s.dtype), shapes)
        return lax.cond(true, f, none, *args)

    def chip(x, k):
        return lax.ppermute(x, "seq", [(s, s ^ (2 * k)) for s in range(count)])

    def sibling(x):
        return lax.ppermute(x, "seq", [(s, s ^ 1) for s in range(count)])

    cross_ks = list(range(far, chips))
    side_groups = [
        [(g * far + j) * 2 + c for j in range(far)] for g in range(2) for c in range(2)
    ]
    side_size = far * slab
    side_start = h // far * side_size
    sizes = [side_size] + [slab] * far

    def send_cross(slabs):
        return {k: chip(slabs[k], k) for k in slabs}

    def send_side(x):
        return lax.all_to_all(
            x, "seq", split_axis=0, concat_axis=0, tiled=True, axis_index_groups=side_groups
        )

    def chip_rows(x, k):
        return lax.dynamic_slice_in_dim(x, jnp.bitwise_xor(h, k) * slab, slab, 0)

    def side_rows(x):
        return lax.dynamic_slice_in_dim(x, side_start, side_size, 0)

    half = chips * share

    def turn(slabs, matrix, side):
        side = send_side(side)
        keep, send = by_columns(functools.partial(split_kernel, share), slabs, [half, half], width, [core])
        other = sibling(send)
        own_out, other_out = by_columns(mix_kernel, [keep, other], [half, half], width, (), [matrix])
        other_in = sibling(other_out)
        sent = by_columns(
            functools.partial(join_kernel, share), [own_out, other_in], sizes, width, [core]
        )
        return side, list(sent), keep, other

    def after(x, earlier):
        return lax.optimization_barrier((x, earlier))

    grads = {k: chip_rows(cotangent, k) * chip_rows(gate_input, k) for k in cross_ks}
    grads, later = after(grads, (cotangent, gate_input, signal))
    side = side_rows(later[0]) * side_rows(later[1])
    grads = send_cross(grads)

    def hot(of, n):
        return (of[:, None] == jnp.arange(n, dtype=jnp.int32)[None, :]).astype(BF16)

    every = jnp.arange(count, dtype=jnp.int32)
    ks = jnp.arange(chips, dtype=jnp.int32)
    order = jnp.where(ks < far, h // far * far + ks, jnp.bitwise_xor(h, ks))
    held = jnp.tile(order, 2) * 2 + jnp.bitwise_xor(e, every // chips)
    relative = jnp.where(ks < far, jnp.bitwise_xor(h % far, ks), ks)
    at = jnp.arange(block, dtype=jnp.int32) % share
    same = at[:, None] == at[None, :]

    def prepare(side, signal, block_factor, cross_factor, order_table, held, order, relative):
        side = send_side(side)
        one_hot = hot(order_table, block)
        permuted = jnp.dot(one_hot, signal, preferred_element_type=F32).astype(BF16)
        within = jnp.tile(jnp.arange(slab, dtype=jnp.int32), chips)
        rows = lambda of: hot(jnp.repeat(of, slab) * slab + within, block)
        factor = jnp.dot(rows(order), block_factor, preferred_element_type=F32).astype(BF16)
        mixed = by_columns(cut_kernel, [permuted], sizes, width, (), [factor])
        home = lax.dot_general(
            one_hot, factor, (((0,), (1,)), ((), ())), preferred_element_type=F32
        ).astype(BF16)
        chosen = hot(held, count)
        near = jnp.einsum("bi,pij->bpj", chosen, cross_factor, preferred_element_type=F32)
        spread_out = jnp.repeat(chosen, share, axis=0)
        cross = jnp.dot(
            near.astype(BF16).reshape(block, count), spread_out.T, preferred_element_type=F32
        )
        cross = jnp.where(same, cross, 0.0).astype(BF16)
        return side, list(mixed), permuted, home, cross, cross.T, chosen, spread_out, rows(relative)

    side, mixed, permuted, home_factor, cross, cross_t, chosen, spread_out, reorder = phase(
        prepare, side, later[2], block_factor, cross_factor, order_table, held, order, relative
    )

    mixed, grads, side = lax.optimization_barrier((mixed, grads, side))
    grads = [side] + [grads[k] for k in cross_ks]
    got = send_cross(dict(zip(cross_ks, mixed[1:])))
    side, back, *grad_rows = phase(turn, grads, cross_t, mixed[0])
    back, got, side = lax.optimization_barrier((back, got, side))
    mixed = [side] + [got[k] for k in cross_ks]

    got = send_cross(dict(zip(cross_ks, back[1:])))
    def cross_gradient(rows, same, chosen, spread_out):
        products = by_columns(
            gradient_kernel,
            rows,
            [(block, count)],
            width,
            whole=[same.astype(BF16), spread_out],
            scratch=[pltpu.VMEM((block, block), F32)],
            dtype=F32,
        )[0]
        return jnp.einsum(
            "bi,bpj->pij",
            chosen.astype(F32),
            products.reshape(count, share, count),
            precision=lax.Precision.HIGHEST,
        ) / math.sqrt(width)

    def turn_and_gradient(slabs, matrix, side, grad_rows, *rest):
        side, sent, *mixed_rows = turn(slabs, matrix, side)
        return side, sent, cross_gradient(grad_rows + mixed_rows, *rest)

    side, gated, grad_cross = phase(
        turn_and_gradient, mixed, cross, back[0], grad_rows, same, chosen, spread_out
    )
    got, side, gated = lax.optimization_barrier((got, side, gated))
    backs = [side] + [got[k] for k in cross_ks]

    gateds = dict(zip(cross_ks, gated[1:]))
    first, second = cross_ks[far // 2 :], cross_ks[: far // 2]
    arrived = send_cross({k: gateds[k] for k in first})

    def home(backs, permuted, home_factor, reorder):
        terms = by_columns(
            partial_kernel,
            [permuted] + backs,
            [(block, block)],
            width,
            whole=[reorder],
            scratch=[pltpu.VMEM((block, block), F32)],
        )[0]
        terms = terms.reshape(chips, 2, share, block)
        mine = lambda i: lax.dynamic_index_in_dim(terms, jnp.bitwise_xor(e, i), 1, keepdims=False)
        terms = tree_sum([mine(0), sibling(mine(1))]).reshape(far, 2, share, block)
        terms = tree_sum([terms[:, 0], chip(terms[:, 1], 1)])
        own = tree_sum([terms[0]] + [chip(terms[k], 2 * k) for k in range(1, far)])
        grad_signal = by_columns(whole_kernel, backs, [block], width, (), [home_factor])[0]
        return own, grad_signal

    own, grad_signal = phase(home, backs, permuted, home_factor, reorder)
    (side, rest), arrived, own = lax.optimization_barrier(
        ((gated[0], {k: gateds[k] for k in second}), arrived, own)
    )
    arrived.update(send_cross({k: rest[k] for k in second[far // 4 :]}))
    side = send_side(side)
    got = [own] + [chip(own, 2 * k) for k in range(1, far)]
    rest, got = after({k: rest[k] for k in second[: far // 4]}, got)
    arrived.update(send_cross(rest))

    def all_rows(got, position):
        near = jnp.stack(got)
        parts = [near, chip(near, 1)]
        parts += [sibling(x) for x in parts]
        return in_order(position, parts, 1.0 / math.sqrt(count * width)).reshape(block, block)

    k = (every % far) * 2 + every // far % 2
    position = jnp.bitwise_xor(h, k) * 2 + jnp.bitwise_xor(e, every // chips)
    grad_block = phase(all_rows, got, position.astype(jnp.int32))
    arrived, side, grad_block = lax.optimization_barrier((arrived, side, grad_block))
    starts = [side_start] + [jnp.bitwise_xor(h, k) * slab for k in cross_ks]
    slabs = [side] + [arrived[k] for k in cross_ks]
    if slab % 16 == 0:
        grad_gate = by_columns(
            place_kernel, [cotangent] + slabs, [block], width, [jnp.stack(starts).astype(jnp.int32)]
        )[0]
    else:
        grad_gate = jnp.zeros_like(cotangent)
        for start, x in zip(starts, slabs):
            rows = lax.dynamic_slice_in_dim(cotangent, start, x.shape[0], 0) * x
            grad_gate = lax.dynamic_update_slice_in_dim(grad_gate, rows, start, 0)
    return (grad_signal, grad_gate, grad_block, grad_cross)


def solution(mesh):
    in_specs = (
        P(("groups", "seq"), None),
        P(("groups", "seq"), None),
        P(("groups", "seq"), None),
        P(),
        P("seq", None, None),
        P(),
    )
    out_specs = (
        P(("groups", "seq"), None),
        P(("groups", "seq"), None),
        P("groups", None),
        P("seq", "groups", None),
    )
    return jax.shard_map(
        per_device, mesh=mesh, in_specs=in_specs, out_specs=out_specs, check_vma=False
    )
```

```python
import functools
import math

import jax
import jax.numpy as jnp
from jax import lax
from jax.experimental import pallas as pl
from jax.experimental.pallas import tpu as pltpu
from jax.sharding import PartitionSpec as P

F32 = jnp.float32
BF16 = jnp.bfloat16
COLUMNS = 512
LIMIT = pltpu.CompilerParams(vmem_limit_bytes=40 * 1024 * 1024)


def split_kernel(share, core, *refs):
    *slabs, keep, send = refs
    mine = core[0] == 0
    at = 0
    for slab in slabs:
        for i in range(0, slab.shape[0], 2 * share):
            low, high = slab[i : i + share], slab[i + share : i + 2 * share]
            keep[at : at + share] = jnp.where(mine, low, high)
            send[at : at + share] = jnp.where(mine, high, low)
            at += share


def join_kernel(share, core, own, other, *slabs):
    mine = core[0] == 0
    at = 0
    for slab in slabs:
        for i in range(0, slab.shape[0], 2 * share):
            a, b = own[at : at + share], other[at : at + share]
            slab[i : i + share] = jnp.where(mine, a, b)
            slab[i + share : i + 2 * share] = jnp.where(mine, b, a)
            at += share


def mix_kernel(matrix, own, other, own_out, other_out):
    rows = jnp.concatenate([own[...], other[...]], axis=0)
    half = own.shape[0]
    own_out[...] = jnp.dot(matrix[:half], rows, preferred_element_type=F32).astype(BF16)
    other_out[...] = jnp.dot(matrix[half:], rows, preferred_element_type=F32).astype(BF16)


def place_kernel(starts, a, *refs):
    *slabs, out = refs
    for i, slab in enumerate(slabs):
        at = pl.ds(pl.multiple_of(starts[i], slab.shape[0]), slab.shape[0])
        out[at] = a[at] * slab[...]


def last_kernel(place, a, slab, old, out):
    out[...] = a[...] * slab[...]


def place_last(place, a, slab, total):
    rows, width = slab.shape
    block = pl.BlockSpec((rows, width), lambda i, place: (place[0], 0))
    return pl.pallas_call(
        last_kernel,
        grid_spec=pltpu.PrefetchScalarGridSpec(
            num_scalar_prefetch=1,
            grid=(1,),
            in_specs=[
                block,
                pl.BlockSpec((rows, width), lambda i, place: (0, 0)),
                pl.BlockSpec(memory_space=pl.ANY),
            ],
            out_specs=block,
        ),
        out_shape=jax.ShapeDtypeStruct(total.shape, BF16),
        input_output_aliases={3: 0},
        compiler_params=LIMIT,
    )(place, a, slab, total)


def cut_kernel(matrix, rows, *slabs):
    total = jnp.dot(matrix[...], rows[...], preferred_element_type=F32).astype(BF16)
    at = 0
    for slab in slabs:
        slab[...] = total[at : at + slab.shape[0]]
        at += slab.shape[0]


def whole_kernel(matrix, *refs):
    *slabs, out = refs
    rows = jnp.concatenate([s[...] for s in slabs], axis=0)
    out[...] = jnp.dot(matrix[...], rows, preferred_element_type=F32).astype(BF16)


def partial_kernel(slab, starts, order, right, side, *refs):
    *slabs, out, total = refs

    @pl.when(pl.program_id(0) == 0)
    def _():
        total[...] = jnp.zeros_like(total)

    count = side.shape[0] // slab
    if slab % 16 == 0:
        rows = [side[pl.ds(pl.multiple_of(starts[k], slab), slab)] for k in range(count)]
    else:
        rows = [side[...]]
    left = jnp.concatenate(rows + [s[...] for s in slabs], axis=0)
    total[...] += lax.dot_general(
        left, right[...], (((1,), (1,)), ((), ())), preferred_element_type=F32
    )

    @pl.when(pl.program_id(0) == pl.num_programs(0) - 1)
    def _():
        if slab % 16 == 0:
            out[...] = total[...]
        else:
            out[...] = jnp.dot(
                order[...].astype(F32),
                total[...],
                precision=lax.Precision.HIGHEST,
                preferred_element_type=F32,
            )


def gradient_kernel(same, spread_out, *refs):
    g, h, m, n, out, total = refs

    @pl.when(pl.program_id(0) == 0)
    def _():
        total[...] = jnp.zeros_like(total)

    left = jnp.concatenate([g[...], h[...]], axis=0)
    right = jnp.concatenate([m[...], n[...]], axis=0)
    total[...] += lax.dot_general(
        left, right, (((1,), (1,)), ((), ())), preferred_element_type=F32
    )

    @pl.when(pl.program_id(0) == pl.num_programs(0) - 1)
    def _():
        out[...] = jnp.dot(
            total[...] * same[...].astype(F32),
            spread_out[...].astype(F32),
            precision=lax.Precision.HIGHEST,
            preferred_element_type=F32,
        )


def order_kernel(scale, position, *refs):
    *parts, out = refs
    at = 0
    for rows in parts:
        for i in range(rows.shape[0]):
            out[position[at]] = rows[i].astype(F32) * scale
            at += 1


def by_columns(kernel, ins, outs, width, scalars=(), whole=(), scratch=(), dtype=BF16):
    columns = min(COLUMNS, width)
    block = lambda rows: pl.BlockSpec((rows, columns), lambda i: (0, i))
    full = lambda shape: pl.BlockSpec(shape, lambda i: (0, 0))
    return pl.pallas_call(
        kernel,
        grid=(width // columns,),
        in_specs=[pl.BlockSpec(memory_space=pltpu.SMEM) for _ in scalars]
        + [full(x.shape) for x in whole]
        + [block(x.shape[0]) for x in ins],
        out_specs=[block(n) if isinstance(n, int) else full(n) for n in outs],
        out_shape=[
            jax.ShapeDtypeStruct((n, width) if isinstance(n, int) else n, dtype) for n in outs
        ],
        scratch_shapes=list(scratch),
        compiler_params=LIMIT,
    )(*scalars, *whole, *ins)


def in_order(position, parts, scale):
    _, share, n = parts[0].shape
    return pl.pallas_call(
        functools.partial(order_kernel, scale),
        in_specs=[pl.BlockSpec(memory_space=pltpu.SMEM)]
        + [pl.BlockSpec(memory_space=pltpu.VMEM) for _ in parts],
        out_specs=pl.BlockSpec(memory_space=pltpu.VMEM),
        out_shape=jax.ShapeDtypeStruct((sum(x.shape[0] for x in parts), share, n), F32),
        compiler_params=LIMIT,
    )(position, *parts)


def per_device(signal, gate_input, cotangent, block_factor, cross_factor, order_table):
    count = lax.axis_size("seq")
    block, width = signal.shape
    share = block // count
    chips, slab = count // 2, 2 * share
    far = chips // 2
    me = lax.axis_index("seq")
    h, e = me // 2, me % 2
    core = e.reshape(1).astype(jnp.int32)
    true = order_table[0] >= 0

    def phase(f, *args):
        shapes = jax.eval_shape(f, *args)
        none = lambda *a: jax.tree.map(lambda s: jnp.zeros(s.shape, s.dtype), shapes)
        return lax.cond(true, f, none, *args)

    def chip(x, k):
        return lax.ppermute(x, "seq", [(s, s ^ (2 * k)) for s in range(count)])

    def near(x, i):
        return lax.ppermute(x, "seq", [(s, s ^ i) for s in range(count)])

    def sibling(x):
        return near(x, 1)

    cross_ks = list(range(far, chips))
    side_groups = [
        [(g * far + j) * 2 + c for j in range(far)] for g in range(2) for c in range(2)
    ]
    side_size = far * slab
    side_start = h // far * side_size
    sizes = [side_size] + [slab] * far

    def send_cross(slabs):
        return {k: chip(slabs[k], k) for k in slabs}

    def send_side(x):
        return lax.all_to_all(
            x, "seq", split_axis=0, concat_axis=0, tiled=True, axis_index_groups=side_groups
        )

    def chip_rows(x, k):
        return lax.dynamic_slice_in_dim(x, jnp.bitwise_xor(h, k) * slab, slab, 0)

    def side_rows(x):
        return lax.dynamic_slice_in_dim(x, side_start, side_size, 0)

    half = chips * share

    def turn(slabs, matrix):
        keep, send = by_columns(functools.partial(split_kernel, share), slabs, [half, half], width, [core])
        other = sibling(send)
        own_out, other_out = by_columns(mix_kernel, [keep, other], [half, half], width, (), [matrix])
        other_in = sibling(other_out)
        sent = by_columns(
            functools.partial(join_kernel, share), [own_out, other_in], sizes, width, [core]
        )
        return list(sent), keep, other

    def after(x, earlier):
        return lax.optimization_barrier((x, earlier))

    grads = {k: chip_rows(cotangent, k) * chip_rows(gate_input, k) for k in cross_ks}
    grads, later = after(grads, (cotangent, gate_input, signal))
    side = side_rows(later[0]) * side_rows(later[1])
    grads = send_cross(grads)

    def hot(of, n):
        return (of[:, None] == jnp.arange(n, dtype=jnp.int32)[None, :]).astype(BF16)

    every = jnp.arange(count, dtype=jnp.int32)
    ks = jnp.arange(chips, dtype=jnp.int32)
    order = jnp.where(ks < far, h // far * far + ks, jnp.bitwise_xor(h, ks))
    held = jnp.tile(order, 2) * 2 + jnp.bitwise_xor(e, every // chips)
    relative = jnp.where(ks < far, jnp.bitwise_xor(h % far, ks), ks)
    at = jnp.arange(block, dtype=jnp.int32) % share
    same = at[:, None] == at[None, :]

    def prepare(signal, block_factor, cross_factor, order_table, held, order, relative):
        one_hot = hot(order_table, block)
        permuted = jnp.dot(one_hot, signal, preferred_element_type=F32).astype(BF16)
        within = jnp.tile(jnp.arange(slab, dtype=jnp.int32), chips)
        rows = lambda of: hot(jnp.repeat(of, slab) * slab + within, block)
        factor = jnp.dot(rows(order), block_factor, preferred_element_type=F32).astype(BF16)
        mixed = by_columns(cut_kernel, [permuted], sizes, width, (), [factor])
        home = lax.dot_general(
            one_hot, factor, (((0,), (1,)), ((), ())), preferred_element_type=F32
        ).astype(BF16)
        chosen = hot(held, count)
        near = jnp.einsum("bi,pij->bpj", chosen, cross_factor, preferred_element_type=F32)
        spread_out = jnp.repeat(chosen, share, axis=0)
        cross = jnp.dot(
            near.astype(BF16).reshape(block, count), spread_out.T, preferred_element_type=F32
        )
        cross = jnp.where(same, cross, 0.0).astype(BF16)
        return list(mixed), permuted, home, cross, cross.T, chosen, spread_out, rows(relative)

    mixed, permuted, home_factor, cross, cross_t, chosen, spread_out, reorder = phase(
        prepare, later[2], block_factor, cross_factor, order_table, held, order, relative
    )

    got = send_cross({far: mixed[1]})
    side, mixed = after(side, mixed)
    side = phase(send_side, side)
    mixed, grads, side = lax.optimization_barrier((mixed, grads, side))
    grads = [side] + [grads[k] for k in cross_ks]
    got.update(send_cross(dict(zip(cross_ks[1:], mixed[2:]))))

    def turn_beside(slabs, matrix, side):
        return send_side(side), *turn(slabs, matrix)

    side, back, *grad_rows = phase(turn_beside, grads, cross_t, mixed[0])
    back, got, side = lax.optimization_barrier((back, got, side))
    mixed = [side] + [got[k] for k in cross_ks]

    got = send_cross(dict(zip(cross_ks, back[1:])))

    def cross_gradient(rows, same, chosen, spread_out):
        products = by_columns(
            gradient_kernel,
            rows,
            [(block, count)],
            width,
            whole=[same.astype(BF16), spread_out],
            scratch=[pltpu.VMEM((block, block), F32)],
            dtype=F32,
        )[0]
        return jnp.einsum(
            "bi,bpj->pij",
            chosen.astype(F32),
            products.reshape(count, share, count),
            precision=lax.Precision.HIGHEST,
        ) / math.sqrt(width)

    def turn_and_gradient(slabs, matrix, side, grad_rows, *rest):
        side = send_side(side)
        sent, *mixed_rows = turn(slabs, matrix)
        return side, sent, cross_gradient(grad_rows + mixed_rows, *rest)

    side, gated, grad_cross = phase(
        turn_and_gradient, mixed, cross, back[0], grad_rows, same, chosen, spread_out
    )
    got, side, gated = lax.optimization_barrier((got, side, gated))
    backs = [side] + [got[k] for k in cross_ks]

    gateds = dict(zip(cross_ks, gated[1:]))
    first, last = cross_ks[::2], cross_ks[1::2]
    arrived = send_cross({k: gateds[k] for k in first})
    gated_side = send_side(gated[0])

    def add(kept, received):
        return sum((x.astype(F32) for x in received), kept)

    def home(backs, permuted, reorder, starts):
        terms = by_columns(
            functools.partial(partial_kernel, slab),
            [permuted] + backs,
            [(block, block)],
            width,
            scalars=[starts],
            whole=[reorder],
            scratch=[pltpu.VMEM((block, block), F32)],
            dtype=F32,
        )[0]
        terms = terms.reshape(far, 2, 2, share, block)
        mine = lambda i: lax.dynamic_index_in_dim(
            terms[:, i // 2], jnp.bitwise_xor(e, i % 2), 1, keepdims=False
        )
        terms = add(mine(0), [near(mine(i).astype(BF16), i) for i in (1, 2, 3)])
        own = add(terms[0], [chip(terms[k].astype(BF16), 2 * k) for k in range(1, far)])
        return own.astype(BF16)

    own = phase(home, backs, permuted, reorder, relative[:far] * slab)
    rest, own, arrived = lax.optimization_barrier(
        ({k: gateds[k] for k in last}, own, arrived)
    )
    got = [own] + [chip(own, 2 * k) for k in range(1, far)]
    rest, got = after(rest, got)
    late = send_cross(rest)

    dynamic = slab % 16 == 0
    starts = {k: jnp.bitwise_xor(h, k) * slab for k in cross_ks}

    def place(total, starts, slabs):
        for start, x in zip(starts, slabs):
            rows = lax.dynamic_slice_in_dim(cotangent, start, x.shape[0], 0) * x
            total = lax.dynamic_update_slice_in_dim(total, rows, start, 0)
        return total

    def finish(got, position, backs, home_factor, cotangent, starts, slabs):
        first = jnp.stack(got)
        rows = in_order(
            position,
            [first] + [near(first, i) for i in (1, 2, 3)],
            1.0 / math.sqrt(count * width),
        )
        grad_signal = by_columns(whole_kernel, backs, [block], width, (), [home_factor])[0]
        if dynamic:
            grad_gate = by_columns(
                place_kernel, [cotangent] + slabs, [block], width, [jnp.stack(starts)]
            )[0]
        else:
            grad_gate = place(jnp.zeros_like(cotangent), starts, slabs)
        return rows.reshape(block, block), grad_signal, grad_gate

    k = every % far * 2 + every // far // 2
    position = jnp.bitwise_xor(h, k) * 2 + jnp.bitwise_xor(e, every // far % 2)
    grad_block, grad_signal, grad_gate = phase(
        finish,
        got,
        position.astype(jnp.int32),
        backs,
        home_factor,
        cotangent,
        [side_start.astype(jnp.int32)] + [starts[k].astype(jnp.int32) for k in first],
        [gated_side] + [arrived[k] for k in first],
    )
    late, grad_gate = after(late, grad_gate)
    if dynamic:
        for k in last:
            at = jnp.bitwise_xor(h, k).reshape(1).astype(jnp.int32)
            grad_gate = place_last(at, cotangent, late[k], grad_gate)
    else:
        grad_gate = place(grad_gate, [starts[k] for k in last], [late[k] for k in last])
    return (grad_signal, grad_gate, grad_block, grad_cross)


def solution(mesh):
    in_specs = (
        P(("groups", "seq"), None),
        P(("groups", "seq"), None),
        P(("groups", "seq"), None),
        P(),
        P("seq", None, None),
        P(),
    )
    out_specs = (
        P(("groups", "seq"), None),
        P(("groups", "seq"), None),
        P("groups", None),
        P("seq", "groups", None),
    )
    return jax.shard_map(
        per_device, mesh=mesh, in_specs=in_specs, out_specs=out_specs, check_vma=False
    )
```

```python
import functools
import math

import jax
import jax.numpy as jnp
from jax import lax
from jax.experimental import pallas as pl
from jax.experimental.pallas import tpu as pltpu
from jax.sharding import PartitionSpec as P

F32 = jnp.float32
BF16 = jnp.bfloat16
COLUMNS = 512
LIMIT = pltpu.CompilerParams(vmem_limit_bytes=40 * 1024 * 1024)


def split_kernel(share, core, *refs):
    *slabs, keep, send = refs
    mine = core[0] == 0
    at = 0
    for slab in slabs:
        for i in range(0, slab.shape[0], 2 * share):
            low, high = slab[i : i + share], slab[i + share : i + 2 * share]
            keep[at : at + share] = jnp.where(mine, low, high)
            send[at : at + share] = jnp.where(mine, high, low)
            at += share


def join_kernel(share, core, own, other, *slabs):
    mine = core[0] == 0
    at = 0
    for slab in slabs:
        for i in range(0, slab.shape[0], 2 * share):
            a, b = own[at : at + share], other[at : at + share]
            slab[i : i + share] = jnp.where(mine, a, b)
            slab[i + share : i + 2 * share] = jnp.where(mine, b, a)
            at += share


def mix_kernel(matrix, own, other, own_out, other_out):
    rows = jnp.concatenate([own[...], other[...]], axis=0)
    half = own.shape[0]
    own_out[...] = jnp.dot(matrix[:half], rows, preferred_element_type=F32).astype(BF16)
    other_out[...] = jnp.dot(matrix[half:], rows, preferred_element_type=F32).astype(BF16)


def place_kernel(starts, a, *refs):
    *slabs, out = refs
    for i, slab in enumerate(slabs):
        at = pl.ds(pl.multiple_of(starts[i], slab.shape[0]), slab.shape[0])
        out[at] = a[at] * slab[...]


def last_kernel(place, a, slab, old, out):
    out[...] = a[...] * slab[...]


def place_last(place, a, slab, total):
    rows, width = slab.shape
    block = pl.BlockSpec((rows, width), lambda i, place: (place[0], 0))
    return pl.pallas_call(
        last_kernel,
        grid_spec=pltpu.PrefetchScalarGridSpec(
            num_scalar_prefetch=1,
            grid=(1,),
            in_specs=[
                block,
                pl.BlockSpec((rows, width), lambda i, place: (0, 0)),
                pl.BlockSpec(memory_space=pl.ANY),
            ],
            out_specs=block,
        ),
        out_shape=jax.ShapeDtypeStruct(total.shape, BF16),
        input_output_aliases={3: 0},
        compiler_params=LIMIT,
    )(place, a, slab, total)


def cut_kernel(matrix, rows, *slabs):
    total = jnp.dot(matrix[...], rows[...], preferred_element_type=F32).astype(BF16)
    at = 0
    for slab in slabs:
        slab[...] = total[at : at + slab.shape[0]]
        at += slab.shape[0]


def whole_kernel(matrix, *refs):
    *slabs, out = refs
    rows = jnp.concatenate([s[...] for s in slabs], axis=0)
    out[...] = jnp.dot(matrix[...], rows, preferred_element_type=F32).astype(BF16)


def partial_kernel(slab, starts, order, right, side, *refs):
    *slabs, out, total = refs

    @pl.when(pl.program_id(0) == 0)
    def _():
        total[...] = jnp.zeros_like(total)

    count = side.shape[0] // slab
    if slab % 16 == 0:
        rows = [side[pl.ds(pl.multiple_of(starts[k], slab), slab)] for k in range(count)]
    else:
        rows = [side[...]]
    left = jnp.concatenate(rows + [s[...] for s in slabs], axis=0)
    total[...] += lax.dot_general(
        left, right[...], (((1,), (1,)), ((), ())), preferred_element_type=F32
    )

    @pl.when(pl.program_id(0) == pl.num_programs(0) - 1)
    def _():
        if slab % 16 == 0:
            out[...] = total[...]
        else:
            out[...] = jnp.dot(
                order[...].astype(F32),
                total[...],
                precision=lax.Precision.HIGHEST,
                preferred_element_type=F32,
            )


def gradient_kernel(same, spread_out, *refs):
    g, h, m, n, out, total = refs

    @pl.when(pl.program_id(0) == 0)
    def _():
        total[...] = jnp.zeros_like(total)

    left = jnp.concatenate([g[...], h[...]], axis=0)
    right = jnp.concatenate([m[...], n[...]], axis=0)
    total[...] += lax.dot_general(
        left, right, (((1,), (1,)), ((), ())), preferred_element_type=F32
    )

    @pl.when(pl.program_id(0) == pl.num_programs(0) - 1)
    def _():
        out[...] = jnp.dot(
            total[...] * same[...].astype(F32),
            spread_out[...].astype(F32),
            precision=lax.Precision.HIGHEST,
            preferred_element_type=F32,
        )


def order_kernel(scale, position, *refs):
    *parts, out = refs
    at = 0
    for rows in parts:
        for i in range(rows.shape[0]):
            out[position[at]] = rows[i].astype(F32) * scale
            at += 1


def by_columns(kernel, ins, outs, width, scalars=(), whole=(), scratch=(), dtype=BF16):
    columns = min(COLUMNS, width)
    block = lambda rows: pl.BlockSpec((rows, columns), lambda i: (0, i))
    full = lambda shape: pl.BlockSpec(shape, lambda i: (0, 0))
    return pl.pallas_call(
        kernel,
        grid=(width // columns,),
        in_specs=[pl.BlockSpec(memory_space=pltpu.SMEM) for _ in scalars]
        + [full(x.shape) for x in whole]
        + [block(x.shape[0]) for x in ins],
        out_specs=[block(n) if isinstance(n, int) else full(n) for n in outs],
        out_shape=[
            jax.ShapeDtypeStruct((n, width) if isinstance(n, int) else n, dtype) for n in outs
        ],
        scratch_shapes=list(scratch),
        compiler_params=LIMIT,
    )(*scalars, *whole, *ins)


def in_order(position, parts, scale):
    _, share, n = parts[0].shape
    return pl.pallas_call(
        functools.partial(order_kernel, scale),
        in_specs=[pl.BlockSpec(memory_space=pltpu.SMEM)]
        + [pl.BlockSpec(memory_space=pltpu.VMEM) for _ in parts],
        out_specs=pl.BlockSpec(memory_space=pltpu.VMEM),
        out_shape=jax.ShapeDtypeStruct((sum(x.shape[0] for x in parts), share, n), F32),
        compiler_params=LIMIT,
    )(position, *parts)


def per_device(signal, gate_input, cotangent, block_factor, cross_factor, order_table):
    count = lax.axis_size("seq")
    block, width = signal.shape
    share = block // count
    chips, slab = count // 2, 2 * share
    far = chips // 2
    me = lax.axis_index("seq")
    h, e = me // 2, me % 2
    core = e.reshape(1).astype(jnp.int32)
    true = order_table[0] >= 0

    def phase(f, *args):
        shapes = jax.eval_shape(f, *args)
        none = lambda *a: jax.tree.map(lambda s: jnp.zeros(s.shape, s.dtype), shapes)
        return lax.cond(true, f, none, *args)

    def chip(x, k):
        return lax.ppermute(x, "seq", [(s, s ^ (2 * k)) for s in range(count)])

    def near(x, i):
        return lax.ppermute(x, "seq", [(s, s ^ i) for s in range(count)])

    def sibling(x):
        return near(x, 1)

    cross_ks = list(range(far, chips))
    side_groups = [
        [(g * far + j) * 2 + c for j in range(far)] for g in range(2) for c in range(2)
    ]
    side_size = far * slab
    side_start = h // far * side_size
    sizes = [side_size] + [slab] * far

    def send_cross(slabs):
        return {k: chip(slabs[k], k) for k in slabs}

    def send_side(x):
        return lax.all_to_all(
            x, "seq", split_axis=0, concat_axis=0, tiled=True, axis_index_groups=side_groups
        )

    def chip_rows(x, k):
        return lax.dynamic_slice_in_dim(x, jnp.bitwise_xor(h, k) * slab, slab, 0)

    def side_rows(x):
        return lax.dynamic_slice_in_dim(x, side_start, side_size, 0)

    half = chips * share

    def turn(slabs, matrix):
        keep, send = by_columns(functools.partial(split_kernel, share), slabs, [half, half], width, [core])
        other = sibling(send)
        own_out, other_out = by_columns(mix_kernel, [keep, other], [half, half], width, (), [matrix])
        other_in = sibling(other_out)
        sent = by_columns(
            functools.partial(join_kernel, share), [own_out, other_in], sizes, width, [core]
        )
        return list(sent), keep, other

    def after(x, earlier):
        return lax.optimization_barrier((x, earlier))

    grads = {k: chip_rows(cotangent, k) * chip_rows(gate_input, k) for k in cross_ks}
    grads, later = after(grads, (cotangent, gate_input, signal))
    side = side_rows(later[0]) * side_rows(later[1])
    grads = send_cross(grads)

    def hot(of, n):
        return (of[:, None] == jnp.arange(n, dtype=jnp.int32)[None, :]).astype(BF16)

    every = jnp.arange(count, dtype=jnp.int32)
    ks = jnp.arange(chips, dtype=jnp.int32)
    order = jnp.where(ks < far, h // far * far + ks, jnp.bitwise_xor(h, ks))
    held = jnp.tile(order, 2) * 2 + jnp.bitwise_xor(e, every // chips)
    relative = jnp.where(ks < far, jnp.bitwise_xor(h % far, ks), ks)
    at = jnp.arange(block, dtype=jnp.int32) % share
    same = at[:, None] == at[None, :]

    def prepare(signal, block_factor, cross_factor, order_table, held, order, relative):
        one_hot = hot(order_table, block)
        permuted = jnp.dot(one_hot, signal, preferred_element_type=F32).astype(BF16)
        within = jnp.tile(jnp.arange(slab, dtype=jnp.int32), chips)
        rows = lambda of: hot(jnp.repeat(of, slab) * slab + within, block)
        factor = jnp.dot(rows(order), block_factor, preferred_element_type=F32).astype(BF16)
        mixed = by_columns(cut_kernel, [permuted], sizes, width, (), [factor])
        home = lax.dot_general(
            one_hot, factor, (((0,), (1,)), ((), ())), preferred_element_type=F32
        ).astype(BF16)
        chosen = hot(held, count)
        near = jnp.einsum("bi,pij->bpj", chosen, cross_factor, preferred_element_type=F32)
        spread_out = jnp.repeat(chosen, share, axis=0)
        cross = jnp.dot(
            near.astype(BF16).reshape(block, count), spread_out.T, preferred_element_type=F32
        )
        cross = jnp.where(same, cross, 0.0).astype(BF16)
        return list(mixed), permuted, home, cross, cross.T, chosen, spread_out, rows(relative)

    mixed, permuted, home_factor, cross, cross_t, chosen, spread_out, reorder = phase(
        prepare, later[2], block_factor, cross_factor, order_table, held, order, relative
    )

    got = send_cross({far: mixed[1]})
    side, mixed = after(side, mixed)
    side = phase(send_side, side)
    mixed, grads, side = lax.optimization_barrier((mixed, grads, side))
    grads = [side] + [grads[k] for k in cross_ks]
    got.update(send_cross(dict(zip(cross_ks[1:], mixed[2:]))))

    def turn_beside(slabs, matrix, side):
        return send_side(side), *turn(slabs, matrix)

    side, back, *grad_rows = phase(turn_beside, grads, cross_t, mixed[0])
    back, got, side = lax.optimization_barrier((back, got, side))
    mixed = [side] + [got[k] for k in cross_ks]

    got = send_cross(dict(zip(cross_ks, back[1:])))

    def cross_gradient(rows, same, chosen, spread_out):
        products = by_columns(
            gradient_kernel,
            rows,
            [(block, count)],
            width,
            whole=[same.astype(BF16), spread_out],
            scratch=[pltpu.VMEM((block, block), F32)],
            dtype=F32,
        )[0]
        return jnp.einsum(
            "bi,bpj->pij",
            chosen.astype(F32),
            products.reshape(count, share, count),
            precision=lax.Precision.HIGHEST,
        ) / math.sqrt(width)

    def turn_and_gradient(slabs, matrix, side, grad_rows, *rest):
        side = send_side(side)
        sent, *mixed_rows = turn(slabs, matrix)
        return side, sent, cross_gradient(grad_rows + mixed_rows, *rest)

    side, gated, grad_cross = phase(
        turn_and_gradient, mixed, cross, back[0], grad_rows, same, chosen, spread_out
    )
    got, side, gated = lax.optimization_barrier((got, side, gated))
    backs = [side] + [got[k] for k in cross_ks]

    gateds = dict(zip(cross_ks, gated[1:]))
    first, last = cross_ks[::2], cross_ks[1::2]
    arrived = send_cross({k: gateds[k] for k in first})

    def add(kept, received):
        return sum((x.astype(F32) for x in received), kept)

    def home(side, backs, permuted, reorder, starts):
        side = send_side(side)
        terms = by_columns(
            functools.partial(partial_kernel, slab),
            [permuted] + backs,
            [(block, block)],
            width,
            scalars=[starts],
            whole=[reorder],
            scratch=[pltpu.VMEM((block, block), F32)],
            dtype=F32,
        )[0]
        terms = terms.reshape(far, 2, 2, share, block)
        mine = lambda i: lax.dynamic_index_in_dim(
            terms[:, i // 2], jnp.bitwise_xor(e, i % 2), 1, keepdims=False
        )
        terms = add(mine(0), [near(mine(i).astype(BF16), i) for i in (1, 2, 3)])
        terms = terms.astype(BF16)
        got = [terms] + [chip(terms, 2 * k) for k in range(1, far)]
        got = [
            jnp.stack([g[k ^ j] for j in range(far)]).astype(F32) if k else g.astype(F32)
            for k, g in enumerate(got)
        ]
        while len(got) > 1:
            got = [x + y for x, y in zip(got[::2], got[1::2])]
        return got[0].astype(BF16), side

    own, gated_side = phase(home, gated[0], backs, permuted, reorder, relative[:far] * slab)
    rest, own, arrived = lax.optimization_barrier(
        ({k: gateds[k] for k in last}, own, arrived)
    )
    late = send_cross(rest)

    dynamic = slab % 16 == 0
    starts = {k: jnp.bitwise_xor(h, k) * slab for k in cross_ks}

    def place(total, starts, slabs):
        for start, x in zip(starts, slabs):
            rows = lax.dynamic_slice_in_dim(cotangent, start, x.shape[0], 0) * x
            total = lax.dynamic_update_slice_in_dim(total, rows, start, 0)
        return total

    def finish(got, position, backs, home_factor, cotangent, starts, slabs):
        rows = in_order(
            position,
            [got] + [near(got, i) for i in (1, 2, 3)],
            1.0 / math.sqrt(count * width),
        )
        grad_signal = by_columns(whole_kernel, backs, [block], width, (), [home_factor])[0]
        if dynamic:
            grad_gate = by_columns(
                place_kernel, [cotangent] + slabs, [block], width, [jnp.stack(starts)]
            )[0]
        else:
            grad_gate = place(jnp.zeros_like(cotangent), starts, slabs)
        return rows.reshape(block, block), grad_signal, grad_gate

    k = every % far * 2 + every // far // 2
    position = jnp.bitwise_xor(h, k) * 2 + jnp.bitwise_xor(e, every // far % 2)
    grad_block, grad_signal, grad_gate = phase(
        finish,
        own,
        position.astype(jnp.int32),
        backs,
        home_factor,
        cotangent,
        [side_start.astype(jnp.int32)] + [starts[k].astype(jnp.int32) for k in first],
        [gated_side] + [arrived[k] for k in first],
    )
    late, grad_gate = after(late, grad_gate)
    if dynamic:
        for k in last:
            at = jnp.bitwise_xor(h, k).reshape(1).astype(jnp.int32)
            grad_gate = place_last(at, cotangent, late[k], grad_gate)
    else:
        grad_gate = place(grad_gate, [starts[k] for k in last], [late[k] for k in last])
    return (grad_signal, grad_gate, grad_block, grad_cross)


def solution(mesh):
    in_specs = (
        P(("groups", "seq"), None),
        P(("groups", "seq"), None),
        P(("groups", "seq"), None),
        P(),
        P("seq", None, None),
        P(),
    )
    out_specs = (
        P(("groups", "seq"), None),
        P(("groups", "seq"), None),
        P("groups", None),
        P("seq", "groups", None),
    )
    return jax.shard_map(
        per_device, mesh=mesh, in_specs=in_specs, out_specs=out_specs, check_vma=False
    )
```

```python
import functools
import math

import jax
import jax.numpy as jnp
from jax import lax
from jax.experimental import pallas as pl
from jax.experimental.pallas import tpu as pltpu
from jax.sharding import PartitionSpec as P

F32 = jnp.float32
BF16 = jnp.bfloat16
COLUMNS = 512
LIMIT = pltpu.CompilerParams(vmem_limit_bytes=40 * 1024 * 1024)


def split_kernel(share, core, *refs):
    *slabs, keep, send = refs
    mine = core[0] == 0
    at = 0
    for slab in slabs:
        for i in range(0, slab.shape[0], 2 * share):
            low, high = slab[i : i + share], slab[i + share : i + 2 * share]
            keep[at : at + share] = jnp.where(mine, low, high)
            send[at : at + share] = jnp.where(mine, high, low)
            at += share


def join_kernel(share, core, own, other, *slabs):
    mine = core[0] == 0
    at = 0
    for slab in slabs:
        for i in range(0, slab.shape[0], 2 * share):
            a, b = own[at : at + share], other[at : at + share]
            slab[i : i + share] = jnp.where(mine, a, b)
            slab[i + share : i + 2 * share] = jnp.where(mine, b, a)
            at += share


def mix_kernel(matrix, own, other, own_out, other_out):
    rows = jnp.concatenate([own[...], other[...]], axis=0)
    half = own.shape[0]
    own_out[...] = jnp.dot(matrix[:half], rows, preferred_element_type=F32).astype(BF16)
    other_out[...] = jnp.dot(matrix[half:], rows, preferred_element_type=F32).astype(BF16)


def place_kernel(starts, a, *refs):
    *slabs, out = refs
    for i, slab in enumerate(slabs):
        at = pl.ds(pl.multiple_of(starts[i], slab.shape[0]), slab.shape[0])
        out[at] = a[at] * slab[...]


def last_kernel(place, a, slab, old, out):
    out[...] = a[...] * slab[...]


def place_last(place, a, slab, total):
    rows, width = slab.shape
    block = pl.BlockSpec((rows, width), lambda i, place: (place[0], 0))
    return pl.pallas_call(
        last_kernel,
        grid_spec=pltpu.PrefetchScalarGridSpec(
            num_scalar_prefetch=1,
            grid=(1,),
            in_specs=[
                block,
                pl.BlockSpec((rows, width), lambda i, place: (0, 0)),
                pl.BlockSpec(memory_space=pl.ANY),
            ],
            out_specs=block,
        ),
        out_shape=pltpu.HBM(total.shape, BF16),
        input_output_aliases={3: 0},
        compiler_params=LIMIT,
    )(place, a, slab, total)


def cut_kernel(matrix, rows, *slabs):
    total = jnp.dot(matrix[...], rows[...], preferred_element_type=F32).astype(BF16)
    at = 0
    for slab in slabs:
        slab[...] = total[at : at + slab.shape[0]]
        at += slab.shape[0]


def whole_kernel(matrix, *refs):
    *slabs, out = refs
    rows = jnp.concatenate([s[...] for s in slabs], axis=0)
    out[...] = jnp.dot(matrix[...], rows, preferred_element_type=F32).astype(BF16)


def partial_kernel(slab, starts, order, right, side, *refs):
    *slabs, out, total = refs

    @pl.when(pl.program_id(0) == 0)
    def _():
        total[...] = jnp.zeros_like(total)

    count = side.shape[0] // slab
    if slab % 16 == 0:
        rows = [side[pl.ds(pl.multiple_of(starts[k], slab), slab)] for k in range(count)]
    else:
        rows = [side[...]]
    left = jnp.concatenate(rows + [s[...] for s in slabs], axis=0)
    total[...] += lax.dot_general(
        left, right[...], (((1,), (1,)), ((), ())), preferred_element_type=F32
    )

    @pl.when(pl.program_id(0) == pl.num_programs(0) - 1)
    def _():
        if slab % 16 == 0:
            out[...] = total[...]
        else:
            out[...] = jnp.dot(
                order[...].astype(F32),
                total[...],
                precision=lax.Precision.HIGHEST,
                preferred_element_type=F32,
            )


def gradient_kernel(same, spread_out, *refs):
    g, h, m, n, out, total = refs

    @pl.when(pl.program_id(0) == 0)
    def _():
        total[...] = jnp.zeros_like(total)

    left = jnp.concatenate([g[...], h[...]], axis=0)
    right = jnp.concatenate([m[...], n[...]], axis=0)
    total[...] += lax.dot_general(
        left, right, (((1,), (1,)), ((), ())), preferred_element_type=F32
    )

    @pl.when(pl.program_id(0) == pl.num_programs(0) - 1)
    def _():
        out[...] = jnp.dot(
            total[...] * same[...].astype(F32),
            spread_out[...].astype(F32),
            precision=lax.Precision.HIGHEST,
            preferred_element_type=F32,
        )


def order_kernel(scale, position, *refs):
    *parts, out = refs
    at = 0
    for rows in parts:
        for i in range(rows.shape[0]):
            out[position[at]] = rows[i].astype(F32) * scale
            at += 1


def by_columns(kernel, ins, outs, width, scalars=(), whole=(), scratch=(), dtype=BF16, result=False):
    columns = min(COLUMNS, width)
    block = lambda rows: pl.BlockSpec((rows, columns), lambda i: (0, i))
    full = lambda shape: pl.BlockSpec(shape, lambda i: (0, 0))
    return pl.pallas_call(
        kernel,
        grid=(width // columns,),
        in_specs=[pl.BlockSpec(memory_space=pltpu.SMEM) for _ in scalars]
        + [full(x.shape) for x in whole]
        + [block(x.shape[0]) for x in ins],
        out_specs=[block(n) if isinstance(n, int) else full(n) for n in outs],
        out_shape=[
            (pltpu.HBM if result else jax.ShapeDtypeStruct)(
                (n, width) if isinstance(n, int) else n, dtype
            )
            for n in outs
        ],
        scratch_shapes=list(scratch),
        compiler_params=LIMIT,
    )(*scalars, *whole, *ins)


def in_order(position, parts, scale):
    _, share, n = parts[0].shape
    return pl.pallas_call(
        functools.partial(order_kernel, scale),
        in_specs=[pl.BlockSpec(memory_space=pltpu.SMEM)]
        + [pl.BlockSpec(memory_space=pltpu.VMEM) for _ in parts],
        out_specs=pl.BlockSpec(memory_space=pltpu.VMEM),
        out_shape=jax.ShapeDtypeStruct((sum(x.shape[0] for x in parts), share, n), F32),
        compiler_params=LIMIT,
    )(position, *parts)


def per_device(signal, gate_input, cotangent, block_factor, cross_factor, order_table):
    count = lax.axis_size("seq")
    block, width = signal.shape
    share = block // count
    chips, slab = count // 2, 2 * share
    far = chips // 2
    me = lax.axis_index("seq")
    h, e = me // 2, me % 2
    core = e.reshape(1).astype(jnp.int32)
    true = order_table[0] >= 0

    def phase(f, *args):
        shapes = jax.eval_shape(f, *args)
        none = lambda *a: jax.tree.map(lambda s: jnp.zeros(s.shape, s.dtype), shapes)
        return lax.cond(true, f, none, *args)

    def chip(x, k):
        return lax.ppermute(x, "seq", [(s, s ^ (2 * k)) for s in range(count)])

    def near(x, i):
        return lax.ppermute(x, "seq", [(s, s ^ i) for s in range(count)])

    def sibling(x):
        return near(x, 1)

    cross_ks = list(range(far, chips))
    side_groups = [
        [(g * far + j) * 2 + c for j in range(far)] for g in range(2) for c in range(2)
    ]
    side_size = far * slab
    side_start = h // far * side_size
    sizes = [side_size] + [slab] * far

    def send_cross(slabs):
        return {k: chip(slabs[k], k) for k in slabs}

    def send_side(x):
        return lax.all_to_all(
            x, "seq", split_axis=0, concat_axis=0, tiled=True, axis_index_groups=side_groups
        )

    def chip_rows(x, k):
        return lax.dynamic_slice_in_dim(x, jnp.bitwise_xor(h, k) * slab, slab, 0)

    def side_rows(x):
        return lax.dynamic_slice_in_dim(x, side_start, side_size, 0)

    half = chips * share

    def turn(slabs, matrix):
        keep, send = by_columns(functools.partial(split_kernel, share), slabs, [half, half], width, [core])
        other = sibling(send)
        own_out, other_out = by_columns(mix_kernel, [keep, other], [half, half], width, (), [matrix])
        other_in = sibling(other_out)
        sent = by_columns(
            functools.partial(join_kernel, share), [own_out, other_in], sizes, width, [core]
        )
        return list(sent), keep, other

    def after(x, earlier):
        return lax.optimization_barrier((x, earlier))

    grads = {k: chip_rows(cotangent, k) * chip_rows(gate_input, k) for k in cross_ks}
    grads, later = after(grads, (cotangent, gate_input, signal))
    side = side_rows(later[0]) * side_rows(later[1])
    grads = send_cross(grads)

    def hot(of, n):
        return (of[:, None] == jnp.arange(n, dtype=jnp.int32)[None, :]).astype(BF16)

    every = jnp.arange(count, dtype=jnp.int32)
    ks = jnp.arange(chips, dtype=jnp.int32)
    order = jnp.where(ks < far, h // far * far + ks, jnp.bitwise_xor(h, ks))
    held = jnp.tile(order, 2) * 2 + jnp.bitwise_xor(e, every // chips)
    relative = jnp.where(ks < far, jnp.bitwise_xor(h % far, ks), ks)
    at = jnp.arange(block, dtype=jnp.int32) % share
    same = at[:, None] == at[None, :]

    def prepare(signal, block_factor, cross_factor, order_table, held, order, relative):
        one_hot = hot(order_table, block)
        permuted = jnp.dot(one_hot, signal, preferred_element_type=F32).astype(BF16)
        within = jnp.tile(jnp.arange(slab, dtype=jnp.int32), chips)
        rows = lambda of: hot(jnp.repeat(of, slab) * slab + within, block)
        factor = jnp.dot(rows(order), block_factor, preferred_element_type=F32).astype(BF16)
        mixed = by_columns(cut_kernel, [permuted], sizes, width, (), [factor])
        home = lax.dot_general(
            one_hot, factor, (((0,), (1,)), ((), ())), preferred_element_type=F32
        ).astype(BF16)
        chosen = hot(held, count)
        near = jnp.einsum("bi,pij->bpj", chosen, cross_factor, preferred_element_type=F32)
        spread_out = jnp.repeat(chosen, share, axis=0)
        cross = jnp.dot(
            near.astype(BF16).reshape(block, count), spread_out.T, preferred_element_type=F32
        )
        cross = jnp.where(same, cross, 0.0).astype(BF16)
        return list(mixed), permuted, home, cross, cross.T, chosen, spread_out, rows(relative)

    mixed, permuted, home_factor, cross, cross_t, chosen, spread_out, reorder = phase(
        prepare, later[2], block_factor, cross_factor, order_table, held, order, relative
    )

    got = send_cross({far: mixed[1]})
    side, mixed = after(side, mixed)
    side = phase(send_side, side)
    mixed, grads, side = lax.optimization_barrier((mixed, grads, side))
    grads = [side] + [grads[k] for k in cross_ks]
    got.update(send_cross(dict(zip(cross_ks[1:], mixed[2:]))))

    def turn_beside(slabs, matrix, side):
        return send_side(side), *turn(slabs, matrix)

    side, back, *grad_rows = phase(turn_beside, grads, cross_t, mixed[0])
    back, got, side = lax.optimization_barrier((back, got, side))
    mixed = [side] + [got[k] for k in cross_ks]

    got = send_cross(dict(zip(cross_ks, back[1:])))

    def cross_gradient(rows, same, chosen, spread_out):
        products = by_columns(
            gradient_kernel,
            rows,
            [(block, count)],
            width,
            whole=[same.astype(BF16), spread_out],
            scratch=[pltpu.VMEM((block, block), F32)],
            dtype=F32,
        )[0]
        return jnp.einsum(
            "bi,bpj->pij",
            chosen.astype(F32),
            products.reshape(count, share, count),
            precision=lax.Precision.HIGHEST,
        ) / math.sqrt(width)

    def turn_and_gradient(slabs, matrix, side, grad_rows, *rest):
        side = send_side(side)
        sent, *mixed_rows = turn(slabs, matrix)
        return side, sent, cross_gradient(grad_rows + mixed_rows, *rest)

    side, gated, grad_cross = phase(
        turn_and_gradient, mixed, cross, back[0], grad_rows, same, chosen, spread_out
    )
    got, side, gated = lax.optimization_barrier((got, side, gated))
    backs = [side] + [got[k] for k in cross_ks]

    gateds = dict(zip(cross_ks, gated[1:]))
    first, last = cross_ks[::2][::-1], cross_ks[1::2][::-1]
    arrived = send_cross({k: gateds[k] for k in first})

    def add(kept, received):
        return sum((x.astype(F32) for x in received), kept)

    def home(side, backs, permuted, reorder, starts):
        side = send_side(side)
        terms = by_columns(
            functools.partial(partial_kernel, slab),
            [permuted] + backs,
            [(block, block)],
            width,
            scalars=[starts],
            whole=[reorder],
            scratch=[pltpu.VMEM((block, block), F32)],
            dtype=F32,
        )[0]
        terms = terms.reshape(far, 2, 2, share, block)
        mine = lambda i: lax.dynamic_index_in_dim(
            terms[:, i // 2], jnp.bitwise_xor(e, i % 2), 1, keepdims=False
        )
        terms = add(mine(0), [near(mine(i).astype(BF16), i) for i in (1, 2, 3)])
        terms = terms.astype(BF16)
        got = [terms] + [chip(terms, 2 * k) for k in range(1, far)]
        got = [
            jnp.stack([g[k ^ j] for j in range(far)]).astype(F32) if k else g.astype(F32)
            for k, g in enumerate(got)
        ]
        while len(got) > 1:
            got = [x + y for x, y in zip(got[::2], got[1::2])]
        return got[0].astype(BF16), side

    own, gated_side = phase(home, gated[0], backs, permuted, reorder, relative[:far] * slab)
    rest, own, arrived = lax.optimization_barrier(
        ({k: gateds[k] for k in last}, own, arrived)
    )
    late = send_cross(rest)

    dynamic = slab % 16 == 0
    starts = {k: jnp.bitwise_xor(h, k) * slab for k in cross_ks}

    def place(total, starts, slabs):
        for start, x in zip(starts, slabs):
            rows = lax.dynamic_slice_in_dim(cotangent, start, x.shape[0], 0) * x
            total = lax.dynamic_update_slice_in_dim(total, rows, start, 0)
        return total

    def finish(got, position, backs, home_factor, cotangent, starts, slabs):
        rows = in_order(
            position,
            [got] + [near(got, i) for i in (1, 2, 3)],
            1.0 / math.sqrt(count * width),
        )
        grad_signal = by_columns(
            whole_kernel, backs, [block], width, (), [home_factor], result=True
        )[0]
        if dynamic:
            grad_gate = by_columns(
                place_kernel,
                [cotangent] + slabs,
                [block],
                width,
                [jnp.stack(starts)],
                result=True,
            )[0]
        else:
            grad_gate = place(jnp.zeros_like(cotangent), starts, slabs)
        return rows.reshape(block, block), grad_signal, grad_gate

    k = every % far * 2 + every // far // 2
    position = jnp.bitwise_xor(h, k) * 2 + jnp.bitwise_xor(e, every // far % 2)
    grad_block, grad_signal, grad_gate = phase(
        finish,
        own,
        position.astype(jnp.int32),
        backs,
        home_factor,
        cotangent,
        [side_start.astype(jnp.int32)] + [starts[k].astype(jnp.int32) for k in first],
        [gated_side] + [arrived[k] for k in first],
    )
    late, grad_gate = after(late, grad_gate)
    if dynamic:
        for k in last:
            at = jnp.bitwise_xor(h, k).reshape(1).astype(jnp.int32)
            grad_gate = place_last(at, cotangent, late[k], grad_gate)
    else:
        grad_gate = place(grad_gate, [starts[k] for k in last], [late[k] for k in last])
    return (grad_signal, grad_gate, grad_block, grad_cross)


def solution(mesh):
    in_specs = (
        P(("groups", "seq"), None),
        P(("groups", "seq"), None),
        P(("groups", "seq"), None),
        P(),
        P("seq", None, None),
        P(),
    )
    out_specs = (
        P(("groups", "seq"), None),
        P(("groups", "seq"), None),
        P("groups", None),
        P("seq", "groups", None),
    )
    return jax.shard_map(
        per_device, mesh=mesh, in_specs=in_specs, out_specs=out_specs, check_vma=False
    )
```

```python
import functools
import math

import jax
import jax.numpy as jnp
from jax import lax
from jax.experimental import pallas as pl
from jax.experimental.pallas import tpu as pltpu
from jax.sharding import PartitionSpec as P

F32 = jnp.float32
BF16 = jnp.bfloat16
COLUMNS = 512
LIMIT = pltpu.CompilerParams(vmem_limit_bytes=40 * 1024 * 1024)


def split_kernel(share, core, *refs):
    *slabs, keep, send = refs
    mine = core[0] == 0
    at = 0
    for slab in slabs:
        for i in range(0, slab.shape[0], 2 * share):
            low, high = slab[i : i + share], slab[i + share : i + 2 * share]
            keep[at : at + share] = jnp.where(mine, low, high)
            send[at : at + share] = jnp.where(mine, high, low)
            at += share


def join_kernel(share, core, own, other, *slabs):
    mine = core[0] == 0
    at = 0
    for slab in slabs:
        for i in range(0, slab.shape[0], 2 * share):
            a, b = own[at : at + share], other[at : at + share]
            slab[i : i + share] = jnp.where(mine, a, b)
            slab[i + share : i + 2 * share] = jnp.where(mine, b, a)
            at += share


def mix_kernel(matrix, own, other, own_out, other_out):
    rows = jnp.concatenate([own[...], other[...]], axis=0)
    half = own.shape[0]
    own_out[...] = jnp.dot(matrix[:half], rows, preferred_element_type=F32).astype(BF16)
    other_out[...] = jnp.dot(matrix[half:], rows, preferred_element_type=F32).astype(BF16)


def place_kernel(starts, a, *refs):
    *slabs, out = refs
    for i, slab in enumerate(slabs):
        at = pl.ds(pl.multiple_of(starts[i], slab.shape[0]), slab.shape[0])
        out[at] = a[at] * slab[...]


def last_kernel(place, a, slab, old, out):
    out[...] = a[...] * slab[...]


def place_last(place, a, slab, total):
    rows, width = slab.shape
    block = pl.BlockSpec((rows, width), lambda i, place: (place[0], 0))
    return pl.pallas_call(
        last_kernel,
        grid_spec=pltpu.PrefetchScalarGridSpec(
            num_scalar_prefetch=1,
            grid=(1,),
            in_specs=[
                block,
                pl.BlockSpec((rows, width), lambda i, place: (0, 0)),
                pl.BlockSpec(memory_space=pl.ANY),
            ],
            out_specs=block,
        ),
        out_shape=pltpu.HBM(total.shape, BF16),
        input_output_aliases={3: 0},
        compiler_params=LIMIT,
    )(place, a, slab, total)


def cut_kernel(matrix, rows, *slabs):
    total = jnp.dot(matrix[...], rows[...], preferred_element_type=F32).astype(BF16)
    at = 0
    for slab in slabs:
        slab[...] = total[at : at + slab.shape[0]]
        at += slab.shape[0]


def whole_kernel(matrix, *refs):
    *slabs, out = refs
    rows = jnp.concatenate([s[...] for s in slabs], axis=0)
    out[...] = jnp.dot(matrix[...], rows, preferred_element_type=F32).astype(BF16)


def partial_kernel(slab, starts, order, right, side, *refs):
    *slabs, out, total = refs

    @pl.when(pl.program_id(0) == 0)
    def _():
        total[...] = jnp.zeros_like(total)

    count = side.shape[0] // slab
    if slab % 16 == 0:
        rows = [side[pl.ds(pl.multiple_of(starts[k], slab), slab)] for k in range(count)]
    else:
        rows = [side[...]]
    left = jnp.concatenate(rows + [s[...] for s in slabs], axis=0)
    total[...] += lax.dot_general(
        left, right[...], (((1,), (1,)), ((), ())), preferred_element_type=F32
    )

    @pl.when(pl.program_id(0) == pl.num_programs(0) - 1)
    def _():
        if slab % 16 == 0:
            out[...] = total[...]
        else:
            out[...] = jnp.dot(
                order[...].astype(F32),
                total[...],
                precision=lax.Precision.HIGHEST,
                preferred_element_type=F32,
            )


def gradient_kernel(same, spread_out, *refs):
    g, h, m, n, out, total = refs

    @pl.when(pl.program_id(0) == 0)
    def _():
        total[...] = jnp.zeros_like(total)

    left = jnp.concatenate([g[...], h[...]], axis=0)
    right = jnp.concatenate([m[...], n[...]], axis=0)
    total[...] += lax.dot_general(
        left, right, (((1,), (1,)), ((), ())), preferred_element_type=F32
    )

    @pl.when(pl.program_id(0) == pl.num_programs(0) - 1)
    def _():
        out[...] = jnp.dot(
            total[...] * same[...].astype(F32),
            spread_out[...].astype(F32),
            precision=lax.Precision.HIGHEST,
            preferred_element_type=F32,
        )


def order_kernel(scale, position, *refs):
    *parts, out = refs
    at = 0
    for rows in parts:
        for i in range(rows.shape[0]):
            out[position[at]] = rows[i].astype(F32) * scale
            at += 1


def by_columns(kernel, ins, outs, width, scalars=(), whole=(), scratch=(), dtype=BF16, result=False):
    columns = min(COLUMNS, width)
    block = lambda rows: pl.BlockSpec((rows, columns), lambda i: (0, i))
    full = lambda shape: pl.BlockSpec(shape, lambda i: (0, 0))
    return pl.pallas_call(
        kernel,
        grid=(width // columns,),
        in_specs=[pl.BlockSpec(memory_space=pltpu.SMEM) for _ in scalars]
        + [full(x.shape) for x in whole]
        + [block(x.shape[0]) for x in ins],
        out_specs=[block(n) if isinstance(n, int) else full(n) for n in outs],
        out_shape=[
            (pltpu.HBM if result else jax.ShapeDtypeStruct)(
                (n, width) if isinstance(n, int) else n, dtype
            )
            for n in outs
        ],
        scratch_shapes=list(scratch),
        compiler_params=LIMIT,
    )(*scalars, *whole, *ins)


def in_order(position, parts, scale):
    _, share, n = parts[0].shape
    return pl.pallas_call(
        functools.partial(order_kernel, scale),
        in_specs=[pl.BlockSpec(memory_space=pltpu.SMEM)]
        + [pl.BlockSpec(memory_space=pltpu.VMEM) for _ in parts],
        out_specs=pl.BlockSpec(memory_space=pltpu.VMEM),
        out_shape=jax.ShapeDtypeStruct((sum(x.shape[0] for x in parts), share, n), F32),
        compiler_params=LIMIT,
    )(position, *parts)


def per_device(signal, gate_input, cotangent, block_factor, cross_factor, order_table):
    count = lax.axis_size("seq")
    block, width = signal.shape
    share = block // count
    chips, slab = count // 2, 2 * share
    far = chips // 2
    me = lax.axis_index("seq")
    h, e = me // 2, me % 2
    core = e.reshape(1).astype(jnp.int32)
    true = order_table[0] >= 0

    def phase(f, *args):
        shapes = jax.eval_shape(f, *args)
        none = lambda *a: jax.tree.map(lambda s: jnp.zeros(s.shape, s.dtype), shapes)
        return lax.cond(true, f, none, *args)

    def chip(x, k):
        return lax.ppermute(x, "seq", [(s, s ^ (2 * k)) for s in range(count)])

    def near(x, i):
        return lax.ppermute(x, "seq", [(s, s ^ i) for s in range(count)])

    def sibling(x):
        return near(x, 1)

    cross_ks = list(range(far, chips))
    side_groups = [
        [(g * far + j) * 2 + c for j in range(far)] for g in range(2) for c in range(2)
    ]
    side_size = far * slab
    side_start = h // far * side_size
    sizes = [side_size] + [slab] * far

    def send_cross(slabs):
        return {k: chip(slabs[k], k) for k in slabs}

    def send_side(x):
        return lax.all_to_all(
            x, "seq", split_axis=0, concat_axis=0, tiled=True, axis_index_groups=side_groups
        )

    def chip_rows(x, k):
        return lax.dynamic_slice_in_dim(x, jnp.bitwise_xor(h, k) * slab, slab, 0)

    def side_rows(x):
        return lax.dynamic_slice_in_dim(x, side_start, side_size, 0)

    half = chips * share

    def turn(slabs, matrix):
        keep, send = by_columns(functools.partial(split_kernel, share), slabs, [half, half], width, [core])
        other = sibling(send)
        own_out, other_out = by_columns(mix_kernel, [keep, other], [half, half], width, (), [matrix])
        other_in = sibling(other_out)
        sent = by_columns(
            functools.partial(join_kernel, share), [own_out, other_in], sizes, width, [core]
        )
        return list(sent), keep, other

    def after(x, earlier):
        return lax.optimization_barrier((x, earlier))

    grads = {k: chip_rows(cotangent, k) * chip_rows(gate_input, k) for k in cross_ks}
    grads, later = after(grads, (cotangent, gate_input, signal))
    side = side_rows(later[0]) * side_rows(later[1])
    grads = send_cross(grads)

    def hot(of, n):
        return (of[:, None] == jnp.arange(n, dtype=jnp.int32)[None, :]).astype(BF16)

    every = jnp.arange(count, dtype=jnp.int32)
    ks = jnp.arange(chips, dtype=jnp.int32)
    order = jnp.where(ks < far, h // far * far + ks, jnp.bitwise_xor(h, ks))
    held = jnp.tile(order, 2) * 2 + jnp.bitwise_xor(e, every // chips)
    relative = jnp.where(ks < far, jnp.bitwise_xor(h % far, ks), ks)
    at = jnp.arange(block, dtype=jnp.int32) % share
    same = at[:, None] == at[None, :]

    def prepare(signal, block_factor, cross_factor, order_table, held, order, relative):
        one_hot = hot(order_table, block)
        permuted = jnp.dot(one_hot, signal, preferred_element_type=F32).astype(BF16)
        within = jnp.tile(jnp.arange(slab, dtype=jnp.int32), chips)
        rows = lambda of: hot(jnp.repeat(of, slab) * slab + within, block)
        factor = jnp.dot(rows(order), block_factor, preferred_element_type=F32).astype(BF16)
        mixed = by_columns(cut_kernel, [permuted], sizes, width, (), [factor])
        home = lax.dot_general(
            one_hot, factor, (((0,), (1,)), ((), ())), preferred_element_type=F32
        ).astype(BF16)
        chosen = hot(held, count)
        near = jnp.einsum("bi,pij->bpj", chosen, cross_factor, preferred_element_type=F32)
        spread_out = jnp.repeat(chosen, share, axis=0)
        cross = jnp.dot(
            near.astype(BF16).reshape(block, count), spread_out.T, preferred_element_type=F32
        )
        cross = jnp.where(same, cross, 0.0).astype(BF16)
        return list(mixed), permuted, home, cross, cross.T, chosen, spread_out, rows(relative)

    mixed, permuted, home_factor, cross, cross_t, chosen, spread_out, reorder = phase(
        prepare, later[2], block_factor, cross_factor, order_table, held, order, relative
    )

    got = send_cross({far: mixed[1]})
    side, mixed = after(side, mixed)
    side = phase(send_side, side)
    mixed, grads, side = lax.optimization_barrier((mixed, grads, side))
    grads = [side] + [grads[k] for k in cross_ks]
    got.update(send_cross(dict(zip(cross_ks[1:], mixed[2:]))))

    def turn_beside(slabs, matrix, side):
        return send_side(side), *turn(slabs, matrix)

    side, back, *grad_rows = phase(turn_beside, grads, cross_t, mixed[0])
    back, got, side = lax.optimization_barrier((back, got, side))
    mixed = [side] + [got[k] for k in cross_ks]

    got = send_cross(dict(zip(cross_ks, back[1:])))

    def cross_gradient(rows, same, chosen, spread_out):
        products = by_columns(
            gradient_kernel,
            rows,
            [(block, count)],
            width,
            whole=[same.astype(BF16), spread_out],
            scratch=[pltpu.VMEM((block, block), F32)],
            dtype=F32,
        )[0]
        return jnp.einsum(
            "bi,bpj->pij",
            chosen.astype(F32),
            products.reshape(count, share, count),
            precision=lax.Precision.HIGHEST,
        ) / math.sqrt(width)

    def turn_and_gradient(slabs, matrix, side, grad_rows, *rest):
        side = send_side(side)
        sent, *mixed_rows = turn(slabs, matrix)
        return side, sent, cross_gradient(grad_rows + mixed_rows, *rest)

    side, gated, grad_cross = phase(
        turn_and_gradient, mixed, cross, back[0], grad_rows, same, chosen, spread_out
    )
    got, side, gated = lax.optimization_barrier((got, side, gated))
    backs = [side] + [got[k] for k in cross_ks]

    gateds = dict(zip(cross_ks, gated[1:]))
    first, last = cross_ks[::2][::-1], cross_ks[1::2][::-1]
    arrived = send_cross({k: gateds[k] for k in first})

    def add(kept, received):
        return sum((x.astype(F32) for x in received), kept)

    def home(side, backs, permuted, reorder, starts):
        side = send_side(side)
        terms = by_columns(
            functools.partial(partial_kernel, slab),
            [permuted] + backs,
            [(block, block)],
            width,
            scalars=[starts],
            whole=[reorder],
            scratch=[pltpu.VMEM((block, block), F32)],
            dtype=F32,
        )[0]
        terms = terms.reshape(far, 2, 2, share, block)
        mine = lambda i: lax.dynamic_index_in_dim(
            terms[:, i // 2], jnp.bitwise_xor(e, i % 2), 1, keepdims=False
        )
        terms = add(mine(0), [near(mine(i).astype(BF16), i) for i in (1, 2, 3)])
        terms = terms.astype(BF16)
        for bit in [1 << i for i in reversed(range(far.bit_length() - 1))]:
            received = chip(terms, 2 * bit)
            received = jnp.stack([received[j ^ bit] for j in range(far)])
            terms = (terms.astype(F32) + received.astype(F32)).astype(BF16)
        return terms, side

    own, gated_side = phase(home, gated[0], backs, permuted, reorder, relative[:far] * slab)
    rest, own, arrived = lax.optimization_barrier(
        ({k: gateds[k] for k in last}, own, arrived)
    )
    late = send_cross(rest)

    dynamic = slab % 16 == 0
    starts = {k: jnp.bitwise_xor(h, k) * slab for k in cross_ks}

    def place(total, starts, slabs):
        for start, x in zip(starts, slabs):
            rows = lax.dynamic_slice_in_dim(cotangent, start, x.shape[0], 0) * x
            total = lax.dynamic_update_slice_in_dim(total, rows, start, 0)
        return total

    def finish(got, position, backs, home_factor, cotangent, starts, slabs):
        rows = in_order(
            position,
            [got] + [near(got, i) for i in (1, 2, 3)],
            1.0 / math.sqrt(count * width),
        )
        grad_signal = by_columns(
            whole_kernel, backs, [block], width, (), [home_factor], result=True
        )[0]
        if dynamic:
            grad_gate = by_columns(
                place_kernel,
                [cotangent] + slabs,
                [block],
                width,
                [jnp.stack(starts)],
                result=True,
            )[0]
        else:
            grad_gate = place(jnp.zeros_like(cotangent), starts, slabs)
        return rows.reshape(block, block), grad_signal, grad_gate

    k = every % far * 2 + every // far // 2
    position = jnp.bitwise_xor(h, k) * 2 + jnp.bitwise_xor(e, every // far % 2)
    grad_block, grad_signal, grad_gate = phase(
        finish,
        own,
        position.astype(jnp.int32),
        backs,
        home_factor,
        cotangent,
        [side_start.astype(jnp.int32)] + [starts[k].astype(jnp.int32) for k in first],
        [gated_side] + [arrived[k] for k in first],
    )
    late, grad_gate = after(late, grad_gate)
    if dynamic:
        for k in last:
            at = jnp.bitwise_xor(h, k).reshape(1).astype(jnp.int32)
            grad_gate = place_last(at, cotangent, late[k], grad_gate)
    else:
        grad_gate = place(grad_gate, [starts[k] for k in last], [late[k] for k in last])
    return (grad_signal, grad_gate, grad_block, grad_cross)


def solution(mesh):
    in_specs = (
        P(("groups", "seq"), None),
        P(("groups", "seq"), None),
        P(("groups", "seq"), None),
        P(),
        P("seq", None, None),
        P(),
    )
    out_specs = (
        P(("groups", "seq"), None),
        P(("groups", "seq"), None),
        P("groups", None),
        P("seq", "groups", None),
    )
    return jax.shard_map(
        per_device, mesh=mesh, in_specs=in_specs, out_specs=out_specs, check_vma=False
    )
```

```python
import functools
import math

import jax
import jax.numpy as jnp
from jax import lax
from jax.experimental import pallas as pl
from jax.experimental.pallas import tpu as pltpu
from jax.sharding import PartitionSpec as P

F32 = jnp.float32
BF16 = jnp.bfloat16
COLUMNS = 1024
LIMIT = pltpu.CompilerParams(vmem_limit_bytes=40 * 1024 * 1024)


def split_kernel(share, core, *refs):
    *slabs, keep, send = refs
    mine = core[0] == 0
    at = 0
    for slab in slabs:
        for i in range(0, slab.shape[0], 2 * share):
            low, high = slab[i : i + share], slab[i + share : i + 2 * share]
            keep[at : at + share] = jnp.where(mine, low, high)
            send[at : at + share] = jnp.where(mine, high, low)
            at += share


def join_kernel(share, core, own, other, *slabs):
    mine = core[0] == 0
    at = 0
    for slab in slabs:
        for i in range(0, slab.shape[0], 2 * share):
            a, b = own[at : at + share], other[at : at + share]
            slab[i : i + share] = jnp.where(mine, a, b)
            slab[i + share : i + 2 * share] = jnp.where(mine, b, a)
            at += share


def mix_kernel(matrix, own, other, own_out, other_out):
    rows = jnp.concatenate([own[...], other[...]], axis=0)
    half = own.shape[0]
    own_out[...] = jnp.dot(matrix[:half], rows, preferred_element_type=F32).astype(BF16)
    other_out[...] = jnp.dot(matrix[half:], rows, preferred_element_type=F32).astype(BF16)


def place_kernel(starts, a, *refs):
    *slabs, out = refs
    for i, slab in enumerate(slabs):
        at = pl.ds(pl.multiple_of(starts[i], slab.shape[0]), slab.shape[0])
        out[at] = a[at] * slab[...]


def last_kernel(place, a, slab, old, out):
    out[...] = a[...] * slab[...]


def place_last(place, a, slab, total):
    rows, width = slab.shape
    block = pl.BlockSpec((rows, width), lambda i, place: (place[0], 0))
    return pl.pallas_call(
        last_kernel,
        grid_spec=pltpu.PrefetchScalarGridSpec(
            num_scalar_prefetch=1,
            grid=(1,),
            in_specs=[
                block,
                pl.BlockSpec((rows, width), lambda i, place: (0, 0)),
                pl.BlockSpec(memory_space=pl.ANY),
            ],
            out_specs=block,
        ),
        out_shape=pltpu.HBM(total.shape, BF16),
        input_output_aliases={3: 0},
        compiler_params=LIMIT,
    )(place, a, slab, total)


def cut_kernel(matrix, rows, *slabs):
    total = jnp.dot(matrix[...], rows[...], preferred_element_type=F32).astype(BF16)
    at = 0
    for slab in slabs:
        slab[...] = total[at : at + slab.shape[0]]
        at += slab.shape[0]


def whole_kernel(matrix, *refs):
    *slabs, out = refs
    rows = jnp.concatenate([s[...] for s in slabs], axis=0)
    out[...] = jnp.dot(matrix[...], rows, preferred_element_type=F32).astype(BF16)


def partial_kernel(slab, starts, order, right, side, *refs):
    *slabs, out, total = refs

    @pl.when(pl.program_id(0) == 0)
    def _():
        total[...] = jnp.zeros_like(total)

    count = side.shape[0] // slab
    if slab % 16 == 0:
        rows = [side[pl.ds(pl.multiple_of(starts[k], slab), slab)] for k in range(count)]
    else:
        rows = [side[...]]
    left = jnp.concatenate(rows + [s[...] for s in slabs], axis=0)
    total[...] += lax.dot_general(
        left, right[...], (((1,), (1,)), ((), ())), preferred_element_type=F32
    )

    @pl.when(pl.program_id(0) == pl.num_programs(0) - 1)
    def _():
        if slab % 16 == 0:
            out[...] = total[...]
        else:
            out[...] = jnp.dot(
                order[...].astype(F32),
                total[...],
                precision=lax.Precision.HIGHEST,
                preferred_element_type=F32,
            )


def gradient_kernel(same, spread_out, *refs):
    g, h, m, n, out, total = refs

    @pl.when(pl.program_id(0) == 0)
    def _():
        total[...] = jnp.zeros_like(total)

    left = jnp.concatenate([g[...], h[...]], axis=0)
    right = jnp.concatenate([m[...], n[...]], axis=0)
    total[...] += lax.dot_general(
        left, right, (((1,), (1,)), ((), ())), preferred_element_type=F32
    )

    @pl.when(pl.program_id(0) == pl.num_programs(0) - 1)
    def _():
        out[...] = jnp.dot(
            total[...] * same[...].astype(F32),
            spread_out[...].astype(F32),
            precision=lax.Precision.HIGHEST,
            preferred_element_type=F32,
        )


def order_kernel(scale, position, *refs):
    *parts, out = refs
    at = 0
    for rows in parts:
        for i in range(rows.shape[0]):
            out[position[at]] = rows[i].astype(F32) * scale
            at += 1


def by_columns(kernel, ins, outs, width, scalars=(), whole=(), scratch=(), dtype=BF16, result=False):
    columns = min(COLUMNS, width)
    block = lambda rows: pl.BlockSpec((rows, columns), lambda i: (0, i))
    full = lambda shape: pl.BlockSpec(shape, lambda i: (0, 0))
    return pl.pallas_call(
        kernel,
        grid=(width // columns,),
        in_specs=[pl.BlockSpec(memory_space=pltpu.SMEM) for _ in scalars]
        + [full(x.shape) for x in whole]
        + [block(x.shape[0]) for x in ins],
        out_specs=[block(n) if isinstance(n, int) else full(n) for n in outs],
        out_shape=[
            (pltpu.HBM if result else jax.ShapeDtypeStruct)(
                (n, width) if isinstance(n, int) else n, dtype
            )
            for n in outs
        ],
        scratch_shapes=list(scratch),
        compiler_params=LIMIT,
    )(*scalars, *whole, *ins)


def in_order(position, parts, scale):
    _, share, n = parts[0].shape
    return pl.pallas_call(
        functools.partial(order_kernel, scale),
        in_specs=[pl.BlockSpec(memory_space=pltpu.SMEM)]
        + [pl.BlockSpec(memory_space=pltpu.VMEM) for _ in parts],
        out_specs=pl.BlockSpec(memory_space=pltpu.VMEM),
        out_shape=jax.ShapeDtypeStruct((sum(x.shape[0] for x in parts), share, n), F32),
        compiler_params=LIMIT,
    )(position, *parts)


def per_device(signal, gate_input, cotangent, block_factor, cross_factor, order_table):
    count = lax.axis_size("seq")
    block, width = signal.shape
    share = block // count
    chips, slab = count // 2, 2 * share
    far = chips // 2
    me = lax.axis_index("seq")
    h, e = me // 2, me % 2
    core = e.reshape(1).astype(jnp.int32)
    true = order_table[0] >= 0

    def phase(f, *args):
        shapes = jax.eval_shape(f, *args)
        none = lambda *a: jax.tree.map(lambda s: jnp.zeros(s.shape, s.dtype), shapes)
        return lax.cond(true, f, none, *args)

    def chip(x, k):
        return lax.ppermute(x, "seq", [(s, s ^ (2 * k)) for s in range(count)])

    def near(x, i):
        return lax.ppermute(x, "seq", [(s, s ^ i) for s in range(count)])

    def sibling(x):
        return near(x, 1)

    cross_ks = list(range(far, chips))
    side_groups = [
        [(g * far + j) * 2 + c for j in range(far)] for g in range(2) for c in range(2)
    ]
    side_size = far * slab
    side_start = h // far * side_size
    sizes = [side_size] + [slab] * far

    def send_cross(slabs):
        return {k: chip(slabs[k], k) for k in slabs}

    def send_side(x):
        return lax.all_to_all(
            x, "seq", split_axis=0, concat_axis=0, tiled=True, axis_index_groups=side_groups
        )

    def chip_rows(x, k):
        return lax.dynamic_slice_in_dim(x, jnp.bitwise_xor(h, k) * slab, slab, 0)

    def side_rows(x):
        return lax.dynamic_slice_in_dim(x, side_start, side_size, 0)

    half = chips * share

    def turn(slabs, matrix):
        keep, send = by_columns(functools.partial(split_kernel, share), slabs, [half, half], width, [core])
        other = sibling(send)
        own_out, other_out = by_columns(mix_kernel, [keep, other], [half, half], width, (), [matrix])
        other_in = sibling(other_out)
        sent = by_columns(
            functools.partial(join_kernel, share), [own_out, other_in], sizes, width, [core]
        )
        return list(sent), keep, other

    def after(x, earlier):
        return lax.optimization_barrier((x, earlier))

    grads = {k: chip_rows(cotangent, k) * chip_rows(gate_input, k) for k in cross_ks}
    grads, later = after(grads, (cotangent, gate_input, signal))
    side = side_rows(later[0]) * side_rows(later[1])
    grads = send_cross(grads)

    def hot(of, n):
        return (of[:, None] == jnp.arange(n, dtype=jnp.int32)[None, :]).astype(BF16)

    every = jnp.arange(count, dtype=jnp.int32)
    ks = jnp.arange(chips, dtype=jnp.int32)
    order = jnp.where(ks < far, h // far * far + ks, jnp.bitwise_xor(h, ks))
    held = jnp.tile(order, 2) * 2 + jnp.bitwise_xor(e, every // chips)
    relative = jnp.where(ks < far, jnp.bitwise_xor(h % far, ks), ks)
    at = jnp.arange(block, dtype=jnp.int32) % share
    same = at[:, None] == at[None, :]

    def prepare(signal, block_factor, cross_factor, order_table, held, order, relative):
        one_hot = hot(order_table, block)
        permuted = jnp.dot(one_hot, signal, preferred_element_type=F32).astype(BF16)
        within = jnp.tile(jnp.arange(slab, dtype=jnp.int32), chips)
        rows = lambda of: hot(jnp.repeat(of, slab) * slab + within, block)
        factor = jnp.dot(rows(order), block_factor, preferred_element_type=F32).astype(BF16)
        mixed = by_columns(cut_kernel, [permuted], sizes, width, (), [factor])
        home = lax.dot_general(
            one_hot, factor, (((0,), (1,)), ((), ())), preferred_element_type=F32
        ).astype(BF16)
        chosen = hot(held, count)
        near = jnp.einsum("bi,pij->bpj", chosen, cross_factor, preferred_element_type=F32)
        spread_out = jnp.repeat(chosen, share, axis=0)
        cross = jnp.dot(
            near.astype(BF16).reshape(block, count), spread_out.T, preferred_element_type=F32
        )
        cross = jnp.where(same, cross, 0.0).astype(BF16)
        return list(mixed), permuted, home, cross, cross.T, chosen, spread_out, rows(relative)

    mixed, permuted, home_factor, cross, cross_t, chosen, spread_out, reorder = phase(
        prepare, later[2], block_factor, cross_factor, order_table, held, order, relative
    )

    got = send_cross({far: mixed[1]})
    side, mixed = after(side, mixed)
    side = phase(send_side, side)
    mixed, grads, side = lax.optimization_barrier((mixed, grads, side))
    grads = [side] + [grads[k] for k in cross_ks]
    got.update(send_cross(dict(zip(cross_ks[1:], mixed[2:]))))

    def turn_beside(slabs, matrix, side):
        return send_side(side), *turn(slabs, matrix)

    side, back, *grad_rows = phase(turn_beside, grads, cross_t, mixed[0])
    back, got, side = lax.optimization_barrier((back, got, side))
    mixed = [side] + [got[k] for k in cross_ks]

    got = send_cross(dict(zip(cross_ks, back[1:])))

    def cross_gradient(rows, same, chosen, spread_out):
        products = by_columns(
            gradient_kernel,
            rows,
            [(block, count)],
            width,
            whole=[same.astype(BF16), spread_out],
            scratch=[pltpu.VMEM((block, block), F32)],
            dtype=F32,
        )[0]
        return jnp.einsum(
            "bi,bpj->pij",
            chosen.astype(F32),
            products.reshape(count, share, count),
            precision=lax.Precision.HIGHEST,
        ) / math.sqrt(width)

    def turn_and_gradient(slabs, matrix, side, grad_rows, *rest):
        side = send_side(side)
        sent, *mixed_rows = turn(slabs, matrix)
        return side, sent, cross_gradient(grad_rows + mixed_rows, *rest)

    side, gated, grad_cross = phase(
        turn_and_gradient, mixed, cross, back[0], grad_rows, same, chosen, spread_out
    )
    got, side, gated = lax.optimization_barrier((got, side, gated))
    backs = [side] + [got[k] for k in cross_ks]

    gateds = dict(zip(cross_ks, gated[1:]))
    first, last = cross_ks[::2][::-1], cross_ks[1::2][::-1]
    arrived = send_cross({k: gateds[k] for k in first})

    def add(kept, received):
        return sum((x.astype(F32) for x in received), kept)

    def home(side, backs, permuted, reorder, starts):
        side = send_side(side)
        terms = by_columns(
            functools.partial(partial_kernel, slab),
            [permuted] + backs,
            [(block, block)],
            width,
            scalars=[starts],
            whole=[reorder],
            scratch=[pltpu.VMEM((block, block), F32)],
            dtype=F32,
        )[0]
        terms = terms.reshape(far, 2, 2, share, block)
        mine = lambda i: lax.dynamic_index_in_dim(
            terms[:, i // 2], jnp.bitwise_xor(e, i % 2), 1, keepdims=False
        )
        terms = add(mine(0), [near(mine(i).astype(BF16), i) for i in (1, 2, 3)])
        terms = terms.astype(BF16)
        for bit in [1 << i for i in reversed(range(far.bit_length() - 1))]:
            received = chip(terms, 2 * bit)
            received = jnp.stack([received[j ^ bit] for j in range(far)])
            terms = (terms.astype(F32) + received.astype(F32)).astype(BF16)
        return terms, side

    own, gated_side = phase(home, gated[0], backs, permuted, reorder, relative[:far] * slab)
    rest, own, arrived = lax.optimization_barrier(
        ({k: gateds[k] for k in last}, own, arrived)
    )
    late = send_cross(rest)

    dynamic = slab % 16 == 0
    starts = {k: jnp.bitwise_xor(h, k) * slab for k in cross_ks}

    def place(total, starts, slabs):
        for start, x in zip(starts, slabs):
            rows = lax.dynamic_slice_in_dim(cotangent, start, x.shape[0], 0) * x
            total = lax.dynamic_update_slice_in_dim(total, rows, start, 0)
        return total

    def finish(got, position, backs, home_factor, cotangent, starts, slabs):
        parts = [got, near(got, 2)]
        parts += [sibling(x) for x in parts]
        rows = in_order(position, parts, 1.0 / math.sqrt(count * width))
        grad_signal = by_columns(
            whole_kernel, backs, [block], width, (), [home_factor], result=True
        )[0]
        if dynamic:
            grad_gate = by_columns(
                place_kernel,
                [cotangent] + slabs,
                [block],
                width,
                [jnp.stack(starts)],
                result=True,
            )[0]
        else:
            grad_gate = place(jnp.zeros_like(cotangent), starts, slabs)
        return rows.reshape(block, block), grad_signal, grad_gate

    k = every % far * 2 + every // far % 2
    position = jnp.bitwise_xor(h, k) * 2 + jnp.bitwise_xor(e, every // chips)
    grad_block, grad_signal, grad_gate = phase(
        finish,
        own,
        position.astype(jnp.int32),
        backs,
        home_factor,
        cotangent,
        [side_start.astype(jnp.int32)] + [starts[k].astype(jnp.int32) for k in first],
        [gated_side] + [arrived[k] for k in first],
    )
    late, grad_gate = after(late, grad_gate)
    if dynamic:
        for k in last:
            at = jnp.bitwise_xor(h, k).reshape(1).astype(jnp.int32)
            grad_gate = place_last(at, cotangent, late[k], grad_gate)
    else:
        grad_gate = place(grad_gate, [starts[k] for k in last], [late[k] for k in last])
    return (grad_signal, grad_gate, grad_block, grad_cross)


def solution(mesh):
    in_specs = (
        P(("groups", "seq"), None),
        P(("groups", "seq"), None),
        P(("groups", "seq"), None),
        P(),
        P("seq", None, None),
        P(),
    )
    out_specs = (
        P(("groups", "seq"), None),
        P(("groups", "seq"), None),
        P("groups", None),
        P("seq", "groups", None),
    )
    return jax.shard_map(
        per_device, mesh=mesh, in_specs=in_specs, out_specs=out_specs, check_vma=False
    )
```
